32 devices in a mesh: seq: 8 (over z, y), tp: 4 (over x, core).
Axes of the slice: x: 2, y: 2, z: 4, core: 2. Of those that a mesh axis runs over, the one named last changes fastest.
Arguments:
- query_in: bfloat16 [1024, 1024], P('seq', 'tp'), may hold values from -6 to 6
- key_in: bfloat16 [1024, 1024], P('seq', 'tp'), may hold values from -6 to 6
- value_in: bfloat16 [1024, 1024], P('seq', 'tp'), may hold values from -6 to 6
- short_weight: float32 [3, 7, 1024], P(None, None, 'tp'), may hold values from -2 to 2
- residue: float32 [16, 1024], P(None, 'tp'), may hold values from -1.5 to 1.5
- rate: float32 [16, 1024], P(None, 'tp'), may hold values from 1e-05 to 0.05
- skip: float32 [1024], P('tp'), may hold values from -4 to 4
- out_weight: bfloat16 [1024, 4096], P('tp'), may hold values from -0.1875 to 0.1875
Outputs:
- mixed: bfloat16 [1024, 4096], P('seq', 'tp')
The draws below stay inside these ranges and needn't reach their ends.
All inputs are finite; a program needn't handle non-finite values.
Results may differ from the reference program's by a relative error of at most 0.0049.
Values may be sent and summed in bfloat16 or wider, within the bound.
A program may use at most 64 MiB of HBM per device.

```python
import math
import jax
import jax.numpy as jnp
from jax import lax

D = 4096
SLAB = 1024
ORDER = 16
KERNEL = 7
TOKENS = 1024


def level_of(stream_key, shape, split, least, high):
    gain, own = 1.0, jax.random.fold_in(stream_key, 6)
    for dim, parts in split:
        steps = jnp.exp(jax.random.uniform(jax.random.fold_in(own, dim), (parts,), jnp.float32, least / len(split), high / len(split)))
        gain = gain * jnp.repeat(steps, shape[dim] // parts).reshape([-1 if axis == dim else 1 for axis in range(len(shape))])
    return gain


def noise(own_key, shape, width, most, pieces=(), kind=jnp.bfloat16):
    array = jax.random.normal(own_key, shape, jnp.float32) * width
    if len(pieces) > 0:
        array = level_of(own_key, shape, pieces, -0.22, 0.18) * array
    return jnp.clip(array, min=-most, max=most).astype(kind)


def setup_inputs(seed: int = 0) -> dict:
    seeds = jax.random.split(jax.random.key(seed), 9)
    query_in = noise(seeds[0], (TOKENS, SLAB), 1.0, 6.0, ((0, 8), (1, 4)))
    key_in = noise(seeds[1], (TOKENS, SLAB), 1.0, 6.0, ((0, 8), (1, 4)))
    value_in = noise(seeds[2], (TOKENS, SLAB), 1.0, 6.0, ((0, 8), (1, 4)))
    short_weight = noise(seeds[3], (3, KERNEL, SLAB), KERNEL ** -0.5, 2.0, ((2, 4),), jnp.float32)
    residue = noise(seeds[4], (ORDER, SLAB), ORDER ** -0.5, 1.5, ((1, 4),), jnp.float32)
    rate = jnp.clip(jnp.exp(math.log(0.05) - 8.517193 * jax.random.uniform(seeds[5], (ORDER, SLAB), jnp.float32) ** level_of(seeds[5], (ORDER, SLAB), ((1, 4),), -0.2, 0.2)), 9.999999747378752e-06, 0.05)
    skip = noise(seeds[6], (SLAB,), 1.0, 4.0, ((0, 4),), jnp.float32)
    out_weight = noise(seeds[7], (SLAB, D), SLAB ** -0.5, 0.1875, ((0, 4),))
    return {"query_in": query_in, "key_in": key_in, "value_in": value_in, "short_weight": short_weight, "residue": residue, "rate": rate, "skip": skip, "out_weight": out_weight}


def short_conv(signal, weights):
    taps = weights.shape[0]
    rows_here = signal.shape[0]
    padded = jnp.concatenate([jnp.zeros((taps - 1, signal.shape[1]), jnp.float32), signal.astype(jnp.float32)], axis=0)
    total = jnp.zeros((rows_here, signal.shape[1]), jnp.float32)
    for offset in range(taps):
        total = total + weights[offset] * padded[taps - 1 - offset:taps - 1 - offset + rows_here]
    return total

def mode_spectrum(rate_block, residue_block, length):
    period = 2 * length
    indices = jnp.arange(period, dtype=jnp.int32)
    angles = (2.0 * math.pi / period * indices.astype(jnp.float32))[:, None]
    parity = (1 - 2 * (indices % 2)).astype(jnp.float32)[:, None]
    spec_real = jnp.zeros((period, rate_block.shape[1]), jnp.float32)
    spec_imag = jnp.zeros((period, rate_block.shape[1]), jnp.float32)
    for order_index in range(rate_block.shape[0]):
        decay = rate_block[order_index]
        retain = jnp.exp(-decay)
        amplitude = residue_block[order_index] * jnp.sqrt(-jnp.expm1(-2.0 * decay))
        leftover = jnp.exp(-decay * length)
        numerator = amplitude * (1.0 - leftover * parity)
        below_real = -jnp.expm1(-decay) + 2.0 * retain * jnp.sin(0.5 * angles) ** 2
        below_imag = retain * jnp.sin(angles)
        below_norm = below_real * below_real + below_imag * below_imag
        spec_real = spec_real + numerator * below_real / below_norm
        spec_imag = spec_imag - numerator * below_imag / below_norm
    return (spec_real, spec_imag)

def reference(query_in, key_in, value_in, short_weight, residue, rate, skip, out_weight):
    queries = short_conv(query_in, short_weight[0])
    keys = short_conv(key_in, short_weight[1])
    values = short_conv(value_in, short_weight[2])
    gated = keys * values
    block = math.gcd(SLAB, 128)
    blocks = SLAB // block

    def block_conv(inputs):
        gated_block, rate_block, residue_block = inputs
        spec_real, spec_imag = mode_spectrum(rate_block, residue_block, TOKENS)
        forward = jnp.fft.fft(gated_block, n=2 * TOKENS, axis=0)
        inverse = jnp.fft.ifft(forward * lax.complex(spec_real, spec_imag), axis=0)
        return jnp.real(inverse[:TOKENS])
    stacked = (gated.reshape(TOKENS, blocks, block).transpose(1, 0, 2), rate.reshape(ORDER, blocks, block).transpose(1, 0, 2), residue.reshape(ORDER, blocks, block).transpose(1, 0, 2))
    longconv = lax.map(block_conv, stacked).transpose(1, 0, 2).reshape(TOKENS, SLAB)
    hyena = (queries * (longconv + skip * gated)).astype(jnp.bfloat16)
    return jnp.dot(hyena, out_weight, preferred_element_type=jnp.float32).astype(jnp.bfloat16)
```

```python
import functools

import jax
import jax.numpy as jnp
from jax import lax
from jax.experimental import pallas as pl
from jax.experimental.pallas import tpu as pltpu
from jax.sharding import PartitionSpec as P

MESH = pl.DeviceIdType.MESH
LANES = 128
SUB = 8
EDGE = 16
CHUNKS = 4


def one_minus_exp_neg(x):
    series = x * (1.0 - x * (1.0 / 2 - x * (1.0 / 6 - x * (1.0 / 24 - x * (1.0 / 120 - x * (1.0 / 720))))))
    return jnp.where(x < 0.2, series, 1.0 - jnp.exp(-x))


def kernel(
    n_seq,
    n_tp,
    query_hbm,
    key_hbm,
    value_hbm,
    taps_hbm,
    residue_hbm,
    rate_hbm,
    skip_hbm,
    weight_hbm,
    out_ref,
    streams,
    taps,
    residue,
    rate,
    skip,
    weight,
    halo,
    extended,
    gext,
    filt,
    conv,
    states,
    own_state,
    queries,
    hyena,
    far_send,
    far_recv,
    near_send,
    near_recv,
    cross_send,
    cross_recv,
    own_part,
    local_sem,
    halo_sem,
    state_send,
    state_recv,
    pair_send,
    pair_recv,
):
    rows, channels = query_hbm.shape
    order = rate_hbm.shape[0]
    n_taps = taps_hbm.shape[1]
    blocks = rows // SUB
    halves = channels // LANES
    width = out_ref.shape[1]
    piece = width // CHUNKS
    me = lax.axis_index("seq")
    tp = lax.axis_index("tp")
    twin = tp + 1 - 2 * lax.rem(tp, 2)
    cross = lax.rem(tp + 2, n_tp)
    twin_cross = lax.rem(twin + 2, n_tp)

    loads = [
        pltpu.make_async_copy(src, dst, local_sem.at[i])
        for i, (src, dst) in enumerate(
            (
                (key_hbm, streams.at[1]),
                (value_hbm, streams.at[2]),
                (query_hbm, streams.at[0]),
                (rate_hbm, rate),
                (residue_hbm, residue),
                (taps_hbm, taps),
                (skip_hbm, skip),
                (weight_hbm, weight),
            )
        )
    ]
    for load in loads:
        load.start()

    barrier = pltpu.get_barrier_semaphore()

    def greet(d, carry):
        pl.semaphore_signal(barrier, inc=1, device_id={"seq": d}, device_id_type=MESH)
        return carry

    lax.fori_loop(0, me, greet, 0)
    for partner in (twin, cross):
        pl.semaphore_signal(barrier, inc=1, device_id={"tp": partner}, device_id_type=MESH)
    for load in loads[:3]:
        load.wait()
    pl.semaphore_wait(barrier, n_seq - 1 - me + 2)

    def halo_copy(i):
        return pltpu.make_async_remote_copy(
            src_ref=streams.at[i, pl.ds(rows - EDGE, EDGE)],
            dst_ref=halo.at[i],
            send_sem=halo_sem.at[i],
            recv_sem=halo_sem.at[3 + i],
            device_id={"seq": lax.rem(me + 1, n_seq)},
            device_id_type=MESH,
        )

    @pl.when(me < n_seq - 1)
    def _():
        for i in (1, 2, 0):
            halo_copy(i).start()

    for load in loads[3:7]:
        load.wait()

    step = lax.broadcasted_iota(jnp.int32, (order, SUB, LANES), 1).astype(jnp.float32)

    def cube(x):
        return jnp.broadcast_to(x[:, None, :], (order, SUB, LANES))

    def amplitude_of(cols):
        return residue[:, cols] * jnp.sqrt(one_minus_exp_neg(2.0 * rate[:, cols]))

    for half in range(halves):
        cols = slice(half * LANES, (half + 1) * LANES)
        rates = cube(rate[:, cols])
        decay = jnp.exp(-float(SUB) * rates)
        term = cube(amplitude_of(cols)) * jnp.exp(-step * rates)
        for b in range(blocks):
            filt[b * SUB : (b + 1) * SUB, cols] = jnp.sum(term, axis=0)
            if b < blocks - 1:
                term = term * decay

    @pl.when(me == 0)
    def _():
        halo[...] = jnp.zeros_like(halo)

    @pl.when(me > 0)
    def _():
        for i in (1, 2, 0):
            halo_copy(i).wait_recv()

    def short_conv(i):
        extended[i, 0:SUB] = halo[i].astype(jnp.float32)[EDGE - SUB :]
        extended[i, SUB:] = streams[i].astype(jnp.float32)
        total = jnp.zeros((rows, channels), jnp.float32)
        for t in range(n_taps):
            total = total + taps[i, t : t + 1, :] * extended[i, SUB - t : SUB - t + rows]
        return total

    gext[0:SUB] = jnp.zeros((SUB, channels), jnp.float32)
    gext[SUB:] = short_conv(1) * short_conv(2)

    for half in range(halves):
        cols = slice(half * LANES, (half + 1) * LANES)
        rates = cube(rate[:, cols])
        decay = jnp.exp(-float(SUB) * rates)
        total = jnp.broadcast_to(gext[SUB : 2 * SUB, cols][None], (order, SUB, LANES))
        for b in range(1, blocks):
            total = total * decay + gext[(b + 1) * SUB : (b + 2) * SUB, cols][None]
        total = total * jnp.exp((step - float(SUB - 1)) * rates)
        own_state[:, cols] = jnp.sum(total, axis=1)

    def state_copy(slot, d):
        return pltpu.make_async_remote_copy(
            src_ref=own_state,
            dst_ref=states.at[slot],
            send_sem=state_send.at[d],
            recv_sem=state_recv.at[slot],
            device_id={"seq": d},
            device_id_type=MESH,
        )

    def send_state(d, carry):
        state_copy(me, d).start()
        return carry

    lax.fori_loop(me + 1, n_seq, send_state, 0)

    queries[...] = short_conv(0)

    def local_conv(half, carry):
        cols = pl.ds(pl.multiple_of(half * LANES, LANES), LANES)
        total = jnp.zeros((rows, LANES), jnp.float32)
        for s in range(SUB):
            shifted = gext[SUB - s : SUB - s + rows, cols]
            for q in range(blocks):
                tap = filt[q * SUB + s : q * SUB + s + 1, cols]
                if q == 0:
                    total = total + tap * shifted
                else:
                    lower = total[q * SUB :] + tap * shifted[: rows - q * SUB]
                    total = jnp.concatenate([total[: q * SUB], lower], axis=0)
        conv[:, cols] = total
        return carry

    lax.fori_loop(0, halves, local_conv, 0)

    span = jnp.exp(-float(rows) * rate[...])

    def take_state(d, held):
        state_copy(d, d).wait_recv()
        return held * span + states[d]

    held = lax.fori_loop(0, me, take_state, jnp.zeros((order, channels), jnp.float32))

    for half in range(halves):
        cols = slice(half * LANES, (half + 1) * LANES)
        rates = cube(rate[:, cols])
        decay = jnp.exp(-float(SUB) * rates)
        term = cube(amplitude_of(cols) * held[:, cols]) * jnp.exp(-(step + 1.0) * rates)
        direct = skip[:, cols]
        for b in range(blocks):
            here = slice(b * SUB, (b + 1) * SUB)
            gated = gext[(b + 1) * SUB : (b + 2) * SUB, cols]
            total = conv[here, cols] + jnp.sum(term, axis=0)
            queries[here, cols] = queries[here, cols] * (total + direct * gated)
            if b < blocks - 1:
                term = term * decay
    hyena[...] = queries[...].astype(jnp.bfloat16)

    loads[7].wait()

    def product(block, c):
        cols = pl.ds(pl.multiple_of(block * width + c * piece, piece), piece)
        return jnp.dot(hyena[...], weight[:, cols], preferred_element_type=jnp.float32)

    def pair_copy(kind, c):
        src, dst, target = (
            (far_send, far_recv, twin),
            (cross_send, cross_recv, cross),
            (near_send, near_recv, twin),
        )[kind]
        return pltpu.make_async_remote_copy(
            src_ref=src.at[c],
            dst_ref=dst.at[c],
            send_sem=pair_send.at[kind * CHUNKS + c],
            recv_sem=pair_recv.at[kind * CHUNKS + c],
            device_id={"tp": target},
            device_id_type=MESH,
        )

    for c in range(CHUNKS):
        far_send[c] = product(twin_cross, c).astype(jnp.bfloat16)
        pair_copy(0, c).start()
    for c in range(CHUNKS):
        mine = product(cross, c)
        pair_copy(0, c).wait_recv()
        cross_send[c] = (mine + far_recv[c].astype(jnp.float32)).astype(jnp.bfloat16)
        pair_copy(1, c).start()
    for c in range(CHUNKS):
        near_send[c] = product(twin, c).astype(jnp.bfloat16)
        pair_copy(2, c).start()
    for c in range(CHUNKS):
        own_part[c] = product(tp, c)
    for c in range(CHUNKS):
        pair_copy(2, c).wait_recv()
        own_part[c] = own_part[c] + near_recv[c].astype(jnp.float32)
    for c in range(CHUNKS):
        pair_copy(1, c).wait_recv()
        total = own_part[c] + cross_recv[c].astype(jnp.float32)
        out_ref[:, c * piece : (c + 1) * piece] = total.astype(out_ref.dtype)

    for kind in range(3):
        for c in range(CHUNKS):
            pair_copy(kind, c).wait_send()

    @pl.when(me < n_seq - 1)
    def _():
        for i in (1, 2, 0):
            halo_copy(i).wait_send()

    def sent_state(d, carry):
        state_copy(me, d).wait_send()
        return carry

    lax.fori_loop(me + 1, n_seq, sent_state, 0)


def solution(mesh):
    n_seq, n_tp = mesh.shape["seq"], mesh.shape["tp"]
    assert n_tp == 4

    def local(query_in, key_in, value_in, short_weight, residue, rate, skip, out_weight):
        rows, channels = query_in.shape
        order, n_taps = rate.shape[0], short_weight.shape[1]
        total_width = out_weight.shape[1]
        width = total_width // n_tp
        piece = width // CHUNKS
        f32, bf16 = jnp.float32, jnp.bfloat16
        pieces = pltpu.VMEM((CHUNKS, rows, piece), bf16)
        return pl.pallas_call(
            functools.partial(kernel, n_seq, n_tp),
            out_shape=jax.ShapeDtypeStruct((rows, width), bf16),
            in_specs=[pl.BlockSpec(memory_space=pl.ANY)] * 8,
            out_specs=pl.BlockSpec(memory_space=pltpu.VMEM),
            scratch_shapes=[
                pltpu.VMEM((3, rows, channels), bf16),
                pltpu.VMEM((3, n_taps, channels), f32),
                pltpu.VMEM((order, channels), f32),
                pltpu.VMEM((order, channels), f32),
                pltpu.VMEM((1, channels), f32),
                pltpu.VMEM((channels, total_width), bf16),
                pltpu.VMEM((3, EDGE, channels), bf16),
                pltpu.VMEM((3, rows + SUB, channels), f32),
                pltpu.VMEM((rows + SUB, channels), f32),
                pltpu.VMEM((rows, channels), f32),
                pltpu.VMEM((rows, channels), f32),
                pltpu.VMEM((n_seq, order, channels), f32),
                pltpu.VMEM((order, channels), f32),
                pltpu.VMEM((rows, channels), f32),
                pltpu.VMEM((rows, channels), bf16),
                pieces,
                pieces,
                pieces,
                pieces,
                pieces,
                pieces,
                pltpu.VMEM((CHUNKS, rows, piece), f32),
                pltpu.SemaphoreType.DMA((8,)),
                pltpu.SemaphoreType.DMA((6,)),
                pltpu.SemaphoreType.DMA((n_seq,)),
                pltpu.SemaphoreType.DMA((n_seq,)),
                pltpu.SemaphoreType.DMA((3 * CHUNKS,)),
                pltpu.SemaphoreType.DMA((3 * CHUNKS,)),
            ],
            compiler_params=pltpu.CompilerParams(
                collective_id=0, has_side_effects=True, vmem_limit_bytes=40 * 1024 * 1024
            ),
        )(
            query_in,
            key_in,
            value_in,
            short_weight,
            residue,
            rate,
            skip.reshape(1, channels),
            out_weight,
        )

    in_specs = (
        P("seq", "tp"),
        P("seq", "tp"),
        P("seq", "tp"),
        P(None, None, "tp"),
        P(None, "tp"),
        P(None, "tp"),
        P("tp"),
        P("tp", None),
    )
    return jax.shard_map(local, mesh=mesh, in_specs=in_specs, out_specs=P("seq", "tp"), check_vma=False)
```

```python
import functools

import jax
import jax.numpy as jnp
from jax import lax
from jax.experimental import pallas as pl
from jax.experimental.pallas import tpu as pltpu
from jax.sharding import PartitionSpec as P

MESH = pl.DeviceIdType.MESH
LANES = 128
SUB = 8
EDGE = 16
CHUNKS = 4


def one_minus_exp_neg(x):
    series = x * (1.0 - x * (1.0 / 2 - x * (1.0 / 6 - x * (1.0 / 24 - x * (1.0 / 120 - x * (1.0 / 720))))))
    return jnp.where(x < 0.2, series, 1.0 - jnp.exp(-x))


def kernel(
    n_seq,
    n_tp,
    query_hbm,
    key_hbm,
    value_hbm,
    taps_hbm,
    residue_hbm,
    rate_hbm,
    skip_hbm,
    weight_hbm,
    out_ref,
    streams,
    taps,
    residue,
    rate,
    skip,
    weight,
    halo,
    extended,
    gext,
    fext,
    conv,
    states,
    own_state,
    heads,
    own_head,
    queries,
    hyena,
    twin_hyena,
    cross_send,
    cross_recv,
    own_part,
    local_sem,
    halo_sem,
    state_send,
    state_recv,
    head_send,
    head_recv,
    twin_sem,
    cross_out,
    cross_in,
):
    rows, channels = query_hbm.shape
    order = rate_hbm.shape[0]
    n_taps = taps_hbm.shape[1]
    blocks = rows // SUB
    halves = channels // LANES
    width = out_ref.shape[1]
    piece = width // CHUNKS
    me = lax.axis_index("seq")
    tp = lax.axis_index("tp")
    twin = tp + 1 - 2 * lax.rem(tp, 2)
    cross = lax.rem(tp + 2, n_tp)
    twin_cross = lax.rem(twin + 2, n_tp)

    def columns(block):
        return pl.ds(pl.multiple_of(block * width, width), width)

    own_rows, twin_rows = pl.ds(0, channels), pl.ds(channels, channels)
    loads = [
        pltpu.make_async_copy(src, dst, local_sem.at[i])
        for i, (src, dst) in enumerate(
            (
                (rate_hbm, rate),
                (residue_hbm, residue),
                (key_hbm, streams.at[1]),
                (value_hbm, streams.at[2]),
                (taps_hbm, taps),
                (query_hbm, streams.at[0]),
                (skip_hbm, skip),
                (weight_hbm.at[:, columns(cross)], weight.at[0, own_rows]),
                (weight_hbm.at[:, columns(tp)], weight.at[1, own_rows]),
            )
        )
    ]
    for load in loads:
        load.start()

    barrier = pltpu.get_barrier_semaphore()

    def greet(d, carry):
        pl.semaphore_signal(barrier, inc=1, device_id={"seq": d}, device_id_type=MESH)
        return carry

    lax.fori_loop(0, me, greet, 0)
    for partner in (twin, cross):
        pl.semaphore_signal(barrier, inc=1, device_id={"tp": partner}, device_id_type=MESH)

    step = lax.broadcasted_iota(jnp.int32, (order, SUB, LANES), 1).astype(jnp.float32)
    lanes = [slice(half * LANES, (half + 1) * LANES) for half in range(halves)]

    def cube(x):
        return jnp.broadcast_to(x[:, None, :], (order, SUB, LANES))

    def amplitude_of(cols):
        return residue[:, cols] * jnp.sqrt(one_minus_exp_neg(2.0 * rate[:, cols]))

    for load in loads[:2]:
        load.wait()
    fext[0:SUB] = jnp.zeros((SUB, channels), jnp.float32)
    for cols in lanes:
        rates = cube(rate[:, cols])
        decay = jnp.exp(-float(SUB) * rates)
        term = cube(amplitude_of(cols)) * jnp.exp(-step * rates)
        for b in range(blocks):
            fext[(b + 1) * SUB : (b + 2) * SUB, cols] = jnp.sum(term, axis=0)
            if b < blocks - 1:
                term = term * decay

    for load in loads[2:6]:
        load.wait()

    def short_conv(i, first, count):
        total = jnp.zeros((count, channels), jnp.float32)
        for t in range(n_taps):
            begin = first + SUB - t
            total = total + taps[i, t : t + 1, :] * extended[i, begin : begin + count]
        return total

    for i in range(3):
        extended[i, SUB:] = streams[i].astype(jnp.float32)
    gext[0 : 2 * SUB] = jnp.zeros((2 * SUB, channels), jnp.float32)
    gext[2 * SUB :] = short_conv(1, SUB, rows - SUB) * short_conv(2, SUB, rows - SUB)

    for cols in lanes:
        rates = cube(rate[:, cols])
        decay = jnp.exp(-float(SUB) * rates)
        total = jnp.broadcast_to(gext[2 * SUB : 3 * SUB, cols][None], (order, SUB, LANES))
        for b in range(2, blocks):
            total = total * decay + gext[(b + 1) * SUB : (b + 2) * SUB, cols][None]
        total = total * jnp.exp((step - float(SUB - 1)) * rates)
        own_state[:, cols] = jnp.sum(total, axis=1)

    pl.semaphore_wait(barrier, n_seq - 1 - me + 2)

    def halo_copy(i):
        return pltpu.make_async_remote_copy(
            src_ref=streams.at[i, pl.ds(rows - EDGE, EDGE)],
            dst_ref=halo.at[i],
            send_sem=halo_sem.at[i],
            recv_sem=halo_sem.at[3 + i],
            device_id={"seq": lax.rem(me + 1, n_seq)},
            device_id_type=MESH,
        )

    def state_copy(slot, d):
        return pltpu.make_async_remote_copy(
            src_ref=own_state,
            dst_ref=states.at[slot],
            send_sem=state_send.at[d],
            recv_sem=state_recv.at[slot],
            device_id={"seq": d},
            device_id_type=MESH,
        )

    def head_copy(slot, d):
        return pltpu.make_async_remote_copy(
            src_ref=own_head,
            dst_ref=heads.at[slot],
            send_sem=head_send.at[d],
            recv_sem=head_recv.at[slot],
            device_id={"seq": d},
            device_id_type=MESH,
        )

    def weight_copy(i):
        return pltpu.make_async_remote_copy(
            src_ref=weight_hbm.at[:, columns((twin_cross, twin)[i])],
            dst_ref=weight.at[i, twin_rows],
            send_sem=twin_sem.at[i],
            recv_sem=twin_sem.at[3 + i],
            device_id={"tp": twin},
            device_id_type=MESH,
        )

    hyena_copy = pltpu.make_async_remote_copy(
        src_ref=hyena,
        dst_ref=twin_hyena,
        send_sem=twin_sem.at[2],
        recv_sem=twin_sem.at[5],
        device_id={"tp": twin},
        device_id_type=MESH,
    )

    def cross_copy(c):
        return pltpu.make_async_remote_copy(
            src_ref=cross_send.at[c],
            dst_ref=cross_recv.at[c],
            send_sem=cross_out.at[c],
            recv_sem=cross_in.at[c],
            device_id={"tp": cross},
            device_id_type=MESH,
        )

    @pl.when(me < n_seq - 1)
    def _():
        for i in (1, 2, 0):
            halo_copy(i).start()

    def send_state(d, carry):
        state_copy(me, d).start()
        return carry

    lax.fori_loop(me + 1, n_seq, send_state, 0)
    for i in range(2):
        weight_copy(i).start()

    def local_conv(half, carry):
        cols = pl.ds(pl.multiple_of(half * LANES, LANES), LANES)
        total = jnp.zeros((rows, LANES), jnp.float32)
        for s in range(SUB):
            shifted = gext[SUB - s : SUB - s + rows, cols]
            for q in range(blocks):
                tap = fext[(q + 1) * SUB + s : (q + 1) * SUB + s + 1, cols]
                if q == 0:
                    total = total + tap * shifted
                else:
                    lower = total[q * SUB :] + tap * shifted[: rows - q * SUB]
                    total = jnp.concatenate([total[: q * SUB], lower], axis=0)
        conv[:, cols] = total
        return carry

    lax.fori_loop(0, halves, local_conv, 0)

    @pl.when(me == 0)
    def _():
        halo[...] = jnp.zeros_like(halo)

    @pl.when(me > 0)
    def _():
        for i in (1, 2, 0):
            halo_copy(i).wait_recv()

    for i in range(3):
        extended[i, 0:SUB] = halo[i].astype(jnp.float32)[EDGE - SUB :]
    head = short_conv(1, 0, SUB) * short_conv(2, 0, SUB)
    own_head[...] = head
    gext[SUB : 2 * SUB] = head

    def send_head(d, carry):
        head_copy(me, d).start()
        return carry

    lax.fori_loop(me + 1, n_seq, send_head, 0)

    queries[...] = short_conv(0, 0, rows)
    for cols in lanes:
        total = conv[:, cols]
        for j in range(SUB):
            total = total + own_head[j : j + 1, cols] * fext[SUB - j : SUB - j + rows, cols]
        conv[:, cols] = total

    loads[6].wait()
    spans = jnp.exp(-float(rows) * rate[...])
    wide = jnp.broadcast_to(spans[:, None, :], (order, SUB, channels))

    def take_state(d, carry):
        held, front = carry
        state_copy(d, d).wait_recv()
        head_copy(d, d).wait_recv()
        return held * spans + states[d], front * wide + heads[d][None]

    held, front = lax.fori_loop(
        0,
        me,
        take_state,
        (
            jnp.zeros((order, channels), jnp.float32),
            jnp.zeros((order, SUB, channels), jnp.float32),
        ),
    )

    for cols in lanes:
        rates = cube(rate[:, cols])
        decay = jnp.exp(-float(SUB) * rates)
        ahead = jnp.exp((step - float(rows - 1)) * rates) * front[:, :, cols]
        carried = amplitude_of(cols) * (held[:, cols] + jnp.sum(ahead, axis=1))
        term = cube(carried) * jnp.exp(-(step + 1.0) * rates)
        direct = skip[:, cols]
        for b in range(blocks):
            here = slice(b * SUB, (b + 1) * SUB)
            gated = gext[(b + 1) * SUB : (b + 2) * SUB, cols]
            total = conv[here, cols] + jnp.sum(term, axis=0)
            queries[here, cols] = queries[here, cols] * (total + direct * gated)
            if b < blocks - 1:
                term = term * decay
    hyena[...] = queries[...].astype(jnp.bfloat16)
    hyena_copy.start()

    def product(rows_of, block, c, part):
        tile = weight[block, part * channels : (part + 1) * channels, c * piece : (c + 1) * piece]
        return jnp.dot(rows_of[...], tile, preferred_element_type=jnp.float32)

    loads[7].wait()
    for c in range(CHUNKS):
        own_part[c] = product(hyena, 0, c, 0)
    weight_copy(0).wait_recv()
    hyena_copy.wait_recv()
    for c in range(CHUNKS):
        cross_send[c] = (own_part[c] + product(twin_hyena, 0, c, 1)).astype(jnp.bfloat16)
        cross_copy(c).start()
    loads[8].wait()
    weight_copy(1).wait_recv()
    for c in range(CHUNKS):
        own_part[c] = product(hyena, 1, c, 0) + product(twin_hyena, 1, c, 1)
    for c in range(CHUNKS):
        cross_copy(c).wait_recv()
        total = own_part[c] + cross_recv[c].astype(jnp.float32)
        out_ref[:, c * piece : (c + 1) * piece] = total.astype(out_ref.dtype)

    for c in range(CHUNKS):
        cross_copy(c).wait_send()
    for i in range(2):
        weight_copy(i).wait_send()
    hyena_copy.wait_send()

    @pl.when(me < n_seq - 1)
    def _():
        for i in (1, 2, 0):
            halo_copy(i).wait_send()

    def sent(d, carry):
        state_copy(me, d).wait_send()
        head_copy(me, d).wait_send()
        return carry

    lax.fori_loop(me + 1, n_seq, sent, 0)


def solution(mesh):
    n_seq, n_tp = mesh.shape["seq"], mesh.shape["tp"]
    assert n_tp == 4

    def local(query_in, key_in, value_in, short_weight, residue, rate, skip, out_weight):
        rows, channels = query_in.shape
        order, n_taps = rate.shape[0], short_weight.shape[1]
        width = out_weight.shape[1] // n_tp
        piece = width // CHUNKS
        f32, bf16 = jnp.float32, jnp.bfloat16
        pieces = pltpu.VMEM((CHUNKS, rows, piece), bf16)
        return pl.pallas_call(
            functools.partial(kernel, n_seq, n_tp),
            out_shape=jax.ShapeDtypeStruct((rows, width), bf16),
            in_specs=[pl.BlockSpec(memory_space=pltpu.HBM)] * 8,
            out_specs=pl.BlockSpec(memory_space=pltpu.VMEM),
            scratch_shapes=[
                pltpu.VMEM((3, rows, channels), bf16),
                pltpu.VMEM((3, n_taps, channels), f32),
                pltpu.VMEM((order, channels), f32),
                pltpu.VMEM((order, channels), f32),
                pltpu.VMEM((1, channels), f32),
                pltpu.VMEM((2, 2 * channels, width), bf16),
                pltpu.VMEM((3, EDGE, channels), bf16),
                pltpu.VMEM((3, rows + SUB, channels), f32),
                pltpu.VMEM((rows + SUB, channels), f32),
                pltpu.VMEM((rows + SUB, channels), f32),
                pltpu.VMEM((rows, channels), f32),
                pltpu.VMEM((n_seq, order, channels), f32),
                pltpu.VMEM((order, channels), f32),
                pltpu.VMEM((n_seq, SUB, channels), f32),
                pltpu.VMEM((SUB, channels), f32),
                pltpu.VMEM((rows, channels), f32),
                pltpu.VMEM((rows, channels), bf16),
                pltpu.VMEM((rows, channels), bf16),
                pieces,
                pieces,
                pltpu.VMEM((CHUNKS, rows, piece), f32),
                pltpu.SemaphoreType.DMA((9,)),
                pltpu.SemaphoreType.DMA((6,)),
                pltpu.SemaphoreType.DMA((n_seq,)),
                pltpu.SemaphoreType.DMA((n_seq,)),
                pltpu.SemaphoreType.DMA((n_seq,)),
                pltpu.SemaphoreType.DMA((n_seq,)),
                pltpu.SemaphoreType.DMA((6,)),
                pltpu.SemaphoreType.DMA((CHUNKS,)),
                pltpu.SemaphoreType.DMA((CHUNKS,)),
            ],
            compiler_params=pltpu.CompilerParams(
                collective_id=0, has_side_effects=True, vmem_limit_bytes=60 * 1024 * 1024
            ),
        )(
            query_in,
            key_in,
            value_in,
            short_weight,
            residue,
            rate,
            skip.reshape(1, channels),
            out_weight,
        )

    in_specs = (
        P("seq", "tp"),
        P("seq", "tp"),
        P("seq", "tp"),
        P(None, None, "tp"),
        P(None, "tp"),
        P(None, "tp"),
        P("tp"),
        P("tp", None),
    )
    return jax.shard_map(local, mesh=mesh, in_specs=in_specs, out_specs=P("seq", "tp"), check_vma=False)
```

```python
import functools

import jax
import jax.numpy as jnp
from jax import lax
from jax.experimental import pallas as pl
from jax.experimental.pallas import tpu as pltpu
from jax.sharding import PartitionSpec as P

MESH = pl.DeviceIdType.MESH
LANES = 128
SUB = 8
EDGE = 16
CHUNKS = 4
EARLY = 2


def one_minus_exp_neg(x):
    series = x * (1.0 - x * (1.0 / 2 - x * (1.0 / 6 - x * (1.0 / 24 - x * (1.0 / 120 - x * (1.0 / 720))))))
    return jnp.where(x < 0.2, series, 1.0 - jnp.exp(-x))


def kernel(
    n_seq,
    n_tp,
    query_hbm,
    key_hbm,
    value_hbm,
    taps_hbm,
    residue_hbm,
    rate_hbm,
    skip_hbm,
    weight_hbm,
    out_hbm,
    streams,
    taps,
    residue,
    rate,
    skip,
    weight,
    cross_weight,
    far_weight,
    halo,
    extended,
    gext,
    fext,
    conv,
    states,
    own_state,
    heads,
    own_head,
    queries,
    hyena,
    twin_hyena,
    cross_hyena,
    far_hyena,
    result,
    cross_send,
    cross_recv,
    own_part,
    local_sem,
    halo_sem,
    state_send,
    state_recv,
    head_send,
    head_recv,
    tp_out,
    tp_in,
    cross_out,
    cross_in,
    result_sem,
):
    rows, channels = query_hbm.shape
    order = rate_hbm.shape[0]
    n_taps = taps_hbm.shape[1]
    blocks = rows // SUB
    halves = channels // LANES
    width = out_hbm.shape[1]
    piece = width // CHUNKS
    me = lax.axis_index("seq")
    tp = lax.axis_index("tp")
    twin = tp + 1 - 2 * lax.rem(tp, 2)
    cross = lax.rem(tp + 2, n_tp)
    twin_cross = lax.rem(twin + 2, n_tp)

    early = EARLY * piece

    def columns(block, first=0, count=width):
        return pl.ds(pl.multiple_of(block * width + first, piece), count)

    own_rows, twin_rows = pl.ds(0, channels), pl.ds(channels, channels)
    loads = [
        pltpu.make_async_copy(src, dst, local_sem.at[i])
        for i, (src, dst) in enumerate(
            (
                (rate_hbm, rate),
                (residue_hbm, residue),
                (key_hbm, streams.at[1]),
                (value_hbm, streams.at[2]),
                (taps_hbm, taps),
                (query_hbm, streams.at[0]),
                (skip_hbm, skip),
                (weight_hbm.at[:, columns(cross, early, width - early)], cross_weight.at[own_rows]),
                (weight_hbm.at[:, columns(tp)], weight.at[own_rows]),
            )
        )
    ]
    for load in loads:
        load.start()

    barrier = pltpu.get_barrier_semaphore()

    def greet(d, carry):
        pl.semaphore_signal(barrier, inc=1, device_id={"seq": d}, device_id_type=MESH)
        return carry

    lax.fori_loop(0, me, greet, 0)
    for partner in (twin, cross, twin_cross):
        pl.semaphore_signal(barrier, inc=1, device_id={"tp": partner}, device_id_type=MESH)

    step = lax.broadcasted_iota(jnp.int32, (order, SUB, LANES), 1).astype(jnp.float32)
    lanes = [slice(half * LANES, (half + 1) * LANES) for half in range(halves)]

    def cube(x):
        return jnp.broadcast_to(x[:, None, :], (order, SUB, LANES))

    def amplitude_of(cols):
        return residue[:, cols] * jnp.sqrt(one_minus_exp_neg(2.0 * rate[:, cols]))

    for load in loads[:2]:
        load.wait()
    fext[0:SUB] = jnp.zeros((SUB, channels), jnp.float32)
    for cols in lanes:
        rates = cube(rate[:, cols])
        decay = jnp.exp(-float(SUB) * rates)
        term = cube(amplitude_of(cols)) * jnp.exp(-step * rates)
        for b in range(blocks):
            fext[(b + 1) * SUB : (b + 2) * SUB, cols] = jnp.sum(term, axis=0)
            if b < blocks - 1:
                term = term * decay

    for load in loads[2:6]:
        load.wait()

    def short_conv(i, first, count):
        total = jnp.zeros((count, channels), jnp.float32)
        for t in range(n_taps):
            begin = first + SUB - t
            total = total + taps[i, t : t + 1, :] * extended[i, begin : begin + count]
        return total

    for i in range(3):
        extended[i, SUB:] = streams[i].astype(jnp.float32)
    gext[0 : 2 * SUB] = jnp.zeros((2 * SUB, channels), jnp.float32)
    gext[2 * SUB :] = short_conv(1, SUB, rows - SUB) * short_conv(2, SUB, rows - SUB)

    for cols in lanes:
        rates = cube(rate[:, cols])
        decay = jnp.exp(-float(SUB) * rates)
        total = jnp.broadcast_to(gext[2 * SUB : 3 * SUB, cols][None], (order, SUB, LANES))
        for b in range(2, blocks):
            total = total * decay + gext[(b + 1) * SUB : (b + 2) * SUB, cols][None]
        total = total * jnp.exp((step - float(SUB - 1)) * rates)
        own_state[:, cols] = jnp.sum(total, axis=1)

    pl.semaphore_wait(barrier, n_seq - 1 - me + 3)

    def halo_copy(i):
        return pltpu.make_async_remote_copy(
            src_ref=streams.at[i, pl.ds(rows - EDGE, EDGE)],
            dst_ref=halo.at[i],
            send_sem=halo_sem.at[i],
            recv_sem=halo_sem.at[3 + i],
            device_id={"seq": lax.rem(me + 1, n_seq)},
            device_id_type=MESH,
        )

    def state_copy(slot, d):
        return pltpu.make_async_remote_copy(
            src_ref=own_state,
            dst_ref=states.at[slot],
            send_sem=state_send.at[d],
            recv_sem=state_recv.at[slot],
            device_id={"seq": d},
            device_id_type=MESH,
        )

    def head_copy(slot, d):
        return pltpu.make_async_remote_copy(
            src_ref=own_head,
            dst_ref=heads.at[slot],
            send_sem=head_send.at[d],
            recv_sem=head_recv.at[slot],
            device_id={"seq": d},
            device_id_type=MESH,
        )

    def tp_copy(i, src, dst, target):
        return pltpu.make_async_remote_copy(
            src_ref=src,
            dst_ref=dst,
            send_sem=tp_out.at[i],
            recv_sem=tp_in.at[i],
            device_id={"tp": target},
            device_id_type=MESH,
        )

    weight_copies = (
        tp_copy(
            0,
            weight_hbm.at[:, columns(twin_cross, early, width - early)],
            cross_weight.at[twin_rows],
            twin,
        ),
        tp_copy(1, weight_hbm.at[:, columns(twin)], weight.at[twin_rows], twin),
        tp_copy(2, weight_hbm.at[:, columns(cross, 0, early)], far_weight.at[own_rows], cross),
        tp_copy(
            3,
            weight_hbm.at[:, columns(twin_cross, 0, early)],
            far_weight.at[twin_rows],
            twin_cross,
        ),
    )
    hyena_cross = tp_copy(4, hyena, cross_hyena, cross)
    hyena_twin = tp_copy(5, hyena, twin_hyena, twin)
    hyena_far = tp_copy(6, cross_hyena, far_hyena, twin)

    def cross_copy(c):
        return pltpu.make_async_remote_copy(
            src_ref=cross_send.at[c],
            dst_ref=cross_recv.at[c],
            send_sem=cross_out.at[c],
            recv_sem=cross_in.at[c],
            device_id={"tp": cross},
            device_id_type=MESH,
        )

    @pl.when(me < n_seq - 1)
    def _():
        for i in (1, 2, 0):
            halo_copy(i).start()

    def send_state(d, carry):
        state_copy(me, d).start()
        return carry

    lax.fori_loop(me + 1, n_seq, send_state, 0)
    for copy in weight_copies:
        copy.start()

    def local_conv(half, carry):
        cols = pl.ds(pl.multiple_of(half * LANES, LANES), LANES)
        total = jnp.zeros((rows, LANES), jnp.float32)
        for s in range(SUB):
            shifted = gext[SUB - s : SUB - s + rows, cols]
            for q in range(blocks):
                tap = fext[(q + 1) * SUB + s : (q + 1) * SUB + s + 1, cols]
                if q == 0:
                    total = total + tap * shifted
                else:
                    lower = total[q * SUB :] + tap * shifted[: rows - q * SUB]
                    total = jnp.concatenate([total[: q * SUB], lower], axis=0)
        conv[:, cols] = total
        return carry

    lax.fori_loop(0, halves, local_conv, 0)

    @pl.when(me == 0)
    def _():
        halo[...] = jnp.zeros_like(halo)

    @pl.when(me > 0)
    def _():
        for i in (1, 2, 0):
            halo_copy(i).wait_recv()

    for i in range(3):
        extended[i, 0:SUB] = halo[i].astype(jnp.float32)[EDGE - SUB :]
    head = short_conv(1, 0, SUB) * short_conv(2, 0, SUB)
    own_head[...] = head
    gext[SUB : 2 * SUB] = head

    def send_head(d, carry):
        head_copy(me, d).start()
        return carry

    lax.fori_loop(me + 1, n_seq, send_head, 0)

    queries[...] = short_conv(0, 0, rows)
    for cols in lanes:
        total = conv[:, cols]
        for j in range(SUB):
            total = total + own_head[j : j + 1, cols] * fext[SUB - j : SUB - j + rows, cols]
        conv[:, cols] = total

    loads[6].wait()
    spans = jnp.exp(-float(rows) * rate[...])
    wide = jnp.broadcast_to(spans[:, None, :], (order, SUB, channels))

    def take_state(d, carry):
        held, front = carry
        state_copy(d, d).wait_recv()
        head_copy(d, d).wait_recv()
        return held * spans + states[d], front * wide + heads[d][None]

    held, front = lax.fori_loop(
        0,
        me,
        take_state,
        (
            jnp.zeros((order, channels), jnp.float32),
            jnp.zeros((order, SUB, channels), jnp.float32),
        ),
    )

    for cols in lanes:
        rates = cube(rate[:, cols])
        decay = jnp.exp(-float(SUB) * rates)
        ahead = jnp.exp((step - float(rows - 1)) * rates) * front[:, :, cols]
        carried = amplitude_of(cols) * (held[:, cols] + jnp.sum(ahead, axis=1))
        term = cube(carried) * jnp.exp(-(step + 1.0) * rates)
        direct = skip[:, cols]
        for b in range(blocks):
            here = slice(b * SUB, (b + 1) * SUB)
            gated = gext[(b + 1) * SUB : (b + 2) * SUB, cols]
            total = conv[here, cols] + jnp.sum(term, axis=0)
            queries[here, cols] = queries[here, cols] * (total + direct * gated)
            if b < blocks - 1:
                term = term * decay
    hyena[...] = queries[...].astype(jnp.bfloat16)
    hyena_cross.start()
    hyena_twin.start()

    def product(rows_of, matrix, part, c):
        tile = matrix[part * channels : (part + 1) * channels, c * piece : (c + 1) * piece]
        return jnp.dot(rows_of[...], tile, preferred_element_type=jnp.float32)

    late = range(CHUNKS - EARLY)
    loads[7].wait()
    for c in late:
        own_part[c] = product(hyena, cross_weight, 0, c)
    weight_copies[0].wait_recv()
    hyena_twin.wait_recv()
    for c in late:
        cross_send[c] = (own_part[c] + product(twin_hyena, cross_weight, 1, c)).astype(jnp.bfloat16)
        cross_copy(c).start()
    loads[8].wait()
    weight_copies[1].wait_recv()
    for c in range(CHUNKS):
        own_part[c] = product(hyena, weight, 0, c) + product(twin_hyena, weight, 1, c)
    hyena_cross.wait_recv()
    hyena_far.start()
    weight_copies[2].wait_recv()
    for c in range(EARLY):
        own_part[c] = own_part[c] + product(cross_hyena, far_weight, 0, c)
    hyena_far.wait_recv()
    weight_copies[3].wait_recv()

    def result_copy(c):
        cols = slice(c * piece, (c + 1) * piece)
        return pltpu.make_async_copy(result.at[c], out_hbm.at[:, cols], result_sem.at[c])

    for c in range(EARLY):
        total = own_part[c] + product(far_hyena, far_weight, 1, c)
        result[c] = total.astype(jnp.bfloat16)
        result_copy(c).start()
    for c in late:
        cross_copy(c).wait_recv()
        total = own_part[EARLY + c] + cross_recv[c].astype(jnp.float32)
        result[EARLY + c] = total.astype(jnp.bfloat16)
        result_copy(EARLY + c).start()

    for c in late:
        cross_copy(c).wait_send()
    for copy in weight_copies + (hyena_cross, hyena_twin, hyena_far):
        copy.wait_send()

    @pl.when(me < n_seq - 1)
    def _():
        for i in (1, 2, 0):
            halo_copy(i).wait_send()

    def sent(d, carry):
        state_copy(me, d).wait_send()
        head_copy(me, d).wait_send()
        return carry

    lax.fori_loop(me + 1, n_seq, sent, 0)
    for c in range(CHUNKS):
        result_copy(c).wait()


def solution(mesh):
    n_seq, n_tp = mesh.shape["seq"], mesh.shape["tp"]
    assert n_tp == 4

    def local(query_in, key_in, value_in, short_weight, residue, rate, skip, out_weight):
        rows, channels = query_in.shape
        order, n_taps = rate.shape[0], short_weight.shape[1]
        width = out_weight.shape[1] // n_tp
        piece = width // CHUNKS
        f32, bf16 = jnp.float32, jnp.bfloat16
        return pl.pallas_call(
            functools.partial(kernel, n_seq, n_tp),
            out_shape=jax.ShapeDtypeStruct((rows, width), bf16),
            in_specs=[pl.BlockSpec(memory_space=pltpu.HBM)] * 8,
            out_specs=pl.BlockSpec(memory_space=pl.ANY),
            scratch_shapes=[
                pltpu.VMEM((3, rows, channels), bf16),
                pltpu.VMEM((3, n_taps, channels), f32),
                pltpu.VMEM((order, channels), f32),
                pltpu.VMEM((order, channels), f32),
                pltpu.VMEM((1, channels), f32),
                pltpu.VMEM((2 * channels, width), bf16),
                pltpu.VMEM((2 * channels, width - EARLY * piece), bf16),
                pltpu.VMEM((2 * channels, EARLY * piece), bf16),
                pltpu.VMEM((3, EDGE, channels), bf16),
                pltpu.VMEM((3, rows + SUB, channels), f32),
                pltpu.VMEM((rows + SUB, channels), f32),
                pltpu.VMEM((rows + SUB, channels), f32),
                pltpu.VMEM((rows, channels), f32),
                pltpu.VMEM((n_seq, order, channels), f32),
                pltpu.VMEM((order, channels), f32),
                pltpu.VMEM((n_seq, SUB, channels), f32),
                pltpu.VMEM((SUB, channels), f32),
                pltpu.VMEM((rows, channels), f32),
                pltpu.VMEM((rows, channels), bf16),
                pltpu.VMEM((rows, channels), bf16),
                pltpu.VMEM((rows, channels), bf16),
                pltpu.VMEM((rows, channels), bf16),
                pltpu.VMEM((CHUNKS, rows, piece), bf16),
                pltpu.VMEM((CHUNKS - EARLY, rows, piece), bf16),
                pltpu.VMEM((CHUNKS - EARLY, rows, piece), bf16),
                pltpu.VMEM((CHUNKS, rows, piece), f32),
                pltpu.SemaphoreType.DMA((9,)),
                pltpu.SemaphoreType.DMA((6,)),
                pltpu.SemaphoreType.DMA((n_seq,)),
                pltpu.SemaphoreType.DMA((n_seq,)),
                pltpu.SemaphoreType.DMA((n_seq,)),
                pltpu.SemaphoreType.DMA((n_seq,)),
                pltpu.SemaphoreType.DMA((7,)),
                pltpu.SemaphoreType.DMA((7,)),
                pltpu.SemaphoreType.DMA((CHUNKS - EARLY,)),
                pltpu.SemaphoreType.DMA((CHUNKS - EARLY,)),
                pltpu.SemaphoreType.DMA((CHUNKS,)),
            ],
            compiler_params=pltpu.CompilerParams(
                collective_id=0, has_side_effects=True, vmem_limit_bytes=60 * 1024 * 1024
            ),
        )(
            query_in,
            key_in,
            value_in,
            short_weight,
            residue,
            rate,
            skip.reshape(1, channels),
            out_weight,
        )

    in_specs = (
        P("seq", "tp"),
        P("seq", "tp"),
        P("seq", "tp"),
        P(None, None, "tp"),
        P(None, "tp"),
        P(None, "tp"),
        P("tp"),
        P("tp", None),
    )
    return jax.shard_map(local, mesh=mesh, in_specs=in_specs, out_specs=P("seq", "tp"), check_vma=False)
```

```python
import functools

import jax
import jax.numpy as jnp
from jax import lax
from jax.experimental import pallas as pl
from jax.experimental.pallas import tpu as pltpu
from jax.sharding import PartitionSpec as P

MESH = pl.DeviceIdType.MESH
LANES = 128
SUB = 8
EDGE = 16
CHUNKS = 4


def one_minus_exp_neg(x):
    series = x * (1.0 - x * (1.0 / 2 - x * (1.0 / 6 - x * (1.0 / 24 - x * (1.0 / 120 - x * (1.0 / 720))))))
    return jnp.where(x < 0.2, series, 1.0 - jnp.exp(-x))


def kernel(
    n_seq,
    n_tp,
    query_hbm,
    key_hbm,
    value_hbm,
    taps_hbm,
    residue_hbm,
    rate_hbm,
    skip_hbm,
    weight_hbm,
    out_hbm,
    streams,
    taps,
    residue,
    rate,
    skip,
    weight,
    halo,
    extended,
    gext,
    fext,
    conv,
    states,
    own_state,
    heads,
    own_head,
    queries,
    hyena,
    twin_hyena,
    result,
    cross_send,
    cross_recv,
    own_part,
    local_sem,
    halo_sem,
    state_send,
    state_recv,
    head_send,
    head_recv,
    twin_sem,
    cross_out,
    cross_in,
    result_sem,
):
    rows, channels = query_hbm.shape
    order = rate_hbm.shape[0]
    n_taps = taps_hbm.shape[1]
    blocks = rows // SUB
    halves = channels // LANES
    width = out_hbm.shape[1]
    piece = width // CHUNKS
    me = lax.axis_index("seq")
    tp = lax.axis_index("tp")
    twin = tp + 1 - 2 * lax.rem(tp, 2)
    cross = lax.rem(tp + 2, n_tp)
    twin_cross = lax.rem(twin + 2, n_tp)

    def columns(block):
        return pl.ds(pl.multiple_of(block * width, width), width)

    own_rows, twin_rows = pl.ds(0, channels), pl.ds(channels, channels)
    loads = [
        pltpu.make_async_copy(src, dst, local_sem.at[i])
        for i, (src, dst) in enumerate(
            (
                (rate_hbm, rate),
                (residue_hbm, residue),
                (key_hbm, streams.at[1]),
                (value_hbm, streams.at[2]),
                (taps_hbm, taps),
                (query_hbm, streams.at[0]),
                (skip_hbm, skip),
                (weight_hbm.at[:, columns(cross)], weight.at[0, own_rows]),
                (weight_hbm.at[:, columns(tp)], weight.at[1, own_rows]),
            )
        )
    ]
    for load in loads:
        load.start()

    barrier = pltpu.get_barrier_semaphore()

    def greet(d, carry):
        pl.semaphore_signal(barrier, inc=1, device_id={"seq": d}, device_id_type=MESH)
        return carry

    lax.fori_loop(0, me, greet, 0)
    for partner in (twin, cross):
        pl.semaphore_signal(barrier, inc=1, device_id={"tp": partner}, device_id_type=MESH)

    step = lax.broadcasted_iota(jnp.int32, (order, SUB, LANES), 1).astype(jnp.float32)
    lanes = [slice(half * LANES, (half + 1) * LANES) for half in range(halves)]

    def cube(x):
        return jnp.broadcast_to(x[:, None, :], (order, SUB, LANES))

    def amplitude_of(cols):
        return residue[:, cols] * jnp.sqrt(one_minus_exp_neg(2.0 * rate[:, cols]))

    for load in loads[:2]:
        load.wait()
    fext[0:SUB] = jnp.zeros((SUB, channels), jnp.float32)
    for cols in lanes:
        rates = cube(rate[:, cols])
        decay = jnp.exp(-float(SUB) * rates)
        term = cube(amplitude_of(cols)) * jnp.exp(-step * rates)
        for b in range(blocks):
            fext[(b + 1) * SUB : (b + 2) * SUB, cols] = jnp.sum(term, axis=0)
            if b < blocks - 1:
                term = term * decay

    for load in loads[2:6]:
        load.wait()

    def short_conv(i, first, count):
        total = jnp.zeros((count, channels), jnp.float32)
        for t in range(n_taps):
            begin = first + SUB - t
            total = total + taps[i, t : t + 1, :] * extended[i, begin : begin + count]
        return total

    for i in range(3):
        extended[i, SUB:] = streams[i].astype(jnp.float32)
    gext[0 : 2 * SUB] = jnp.zeros((2 * SUB, channels), jnp.float32)
    gext[2 * SUB :] = short_conv(1, SUB, rows - SUB) * short_conv(2, SUB, rows - SUB)

    for cols in lanes:
        rates = cube(rate[:, cols])
        decay = jnp.exp(-float(SUB) * rates)
        total = jnp.broadcast_to(gext[2 * SUB : 3 * SUB, cols][None], (order, SUB, LANES))
        for b in range(2, blocks):
            total = total * decay + gext[(b + 1) * SUB : (b + 2) * SUB, cols][None]
        total = total * jnp.exp((step - float(SUB - 1)) * rates)
        own_state[:, cols] = jnp.sum(total, axis=1).astype(jnp.bfloat16)

    pl.semaphore_wait(barrier, n_seq - 1 - me + 2)

    def halo_copy(i):
        return pltpu.make_async_remote_copy(
            src_ref=streams.at[i, pl.ds(rows - EDGE, EDGE)],
            dst_ref=halo.at[i],
            send_sem=halo_sem.at[i],
            recv_sem=halo_sem.at[3 + i],
            device_id={"seq": lax.rem(me + 1, n_seq)},
            device_id_type=MESH,
        )

    def state_copy(slot, d):
        return pltpu.make_async_remote_copy(
            src_ref=own_state,
            dst_ref=states.at[slot],
            send_sem=state_send.at[d],
            recv_sem=state_recv.at[slot],
            device_id={"seq": d},
            device_id_type=MESH,
        )

    def head_copy(slot, d):
        return pltpu.make_async_remote_copy(
            src_ref=own_head,
            dst_ref=heads.at[slot],
            send_sem=head_send.at[d],
            recv_sem=head_recv.at[slot],
            device_id={"seq": d},
            device_id_type=MESH,
        )

    def weight_copy(i):
        return pltpu.make_async_remote_copy(
            src_ref=weight_hbm.at[:, columns((twin_cross, twin)[i])],
            dst_ref=weight.at[i, twin_rows],
            send_sem=twin_sem.at[i],
            recv_sem=twin_sem.at[3 + i],
            device_id={"tp": twin},
            device_id_type=MESH,
        )

    hyena_copy = pltpu.make_async_remote_copy(
        src_ref=hyena,
        dst_ref=twin_hyena,
        send_sem=twin_sem.at[2],
        recv_sem=twin_sem.at[5],
        device_id={"tp": twin},
        device_id_type=MESH,
    )

    def cross_copy(c):
        return pltpu.make_async_remote_copy(
            src_ref=cross_send.at[c],
            dst_ref=cross_recv.at[c],
            send_sem=cross_out.at[c],
            recv_sem=cross_in.at[c],
            device_id={"tp": cross},
            device_id_type=MESH,
        )

    @pl.when(me < n_seq - 1)
    def _():
        for i in (1, 2, 0):
            halo_copy(i).start()

    def send_state(i, carry):
        state_copy(me, n_seq - 1 - i).start()
        return carry

    lax.fori_loop(0, n_seq - 1 - me, send_state, 0)
    for i in range(2):
        weight_copy(i).start()

    def local_conv(half, carry):
        cols = pl.ds(pl.multiple_of(half * LANES, LANES), LANES)
        total = jnp.zeros((rows, LANES), jnp.float32)
        for s in range(SUB):
            shifted = gext[SUB - s : SUB - s + rows, cols]
            for q in range(blocks):
                tap = fext[(q + 1) * SUB + s : (q + 1) * SUB + s + 1, cols]
                if q == 0:
                    total = total + tap * shifted
                else:
                    lower = total[q * SUB :] + tap * shifted[: rows - q * SUB]
                    total = jnp.concatenate([total[: q * SUB], lower], axis=0)
        conv[:, cols] = total
        return carry

    lax.fori_loop(0, halves, local_conv, 0)

    @pl.when(me == 0)
    def _():
        halo[...] = jnp.zeros_like(halo)

    @pl.when(me > 0)
    def _():
        for i in (1, 2, 0):
            halo_copy(i).wait_recv()

    for i in range(3):
        extended[i, 0:SUB] = halo[i].astype(jnp.float32)[EDGE - SUB :]
    head = short_conv(1, 0, SUB) * short_conv(2, 0, SUB)
    stacked = jnp.concatenate([head[:, cols] for cols in lanes], axis=0)
    own_head[...] = stacked.astype(jnp.bfloat16)
    gext[SUB : 2 * SUB] = head

    def send_head(i, carry):
        head_copy(me, n_seq - 1 - i).start()
        return carry

    lax.fori_loop(0, n_seq - 1 - me, send_head, 0)

    queries[...] = short_conv(0, 0, rows)
    for cols in lanes:
        total = conv[:, cols]
        for j in range(SUB):
            total = total + gext[SUB + j : SUB + j + 1, cols] * fext[SUB - j : SUB - j + rows, cols]
        conv[:, cols] = total

    loads[6].wait()
    spans = jnp.exp(-float(rows) * rate[...])
    wide = jnp.broadcast_to(spans[:, None, :], (order, SUB, channels))

    def take_state(d, carry):
        held, front = carry
        state_copy(d, d).wait_recv()
        head_copy(d, d).wait_recv()
        stacked = heads[d].astype(jnp.float32)
        head = jnp.concatenate(
            [stacked[half * SUB : (half + 1) * SUB] for half in range(halves)], axis=1
        )
        return held * spans + states[d].astype(jnp.float32), front * wide + head[None]

    held, front = lax.fori_loop(
        0,
        me,
        take_state,
        (
            jnp.zeros((order, channels), jnp.float32),
            jnp.zeros((order, SUB, channels), jnp.float32),
        ),
    )

    for cols in lanes:
        rates = cube(rate[:, cols])
        decay = jnp.exp(-float(SUB) * rates)
        ahead = jnp.exp((step - float(rows - 1)) * rates) * front[:, :, cols]
        carried = amplitude_of(cols) * (held[:, cols] + jnp.sum(ahead, axis=1))
        term = cube(carried) * jnp.exp(-(step + 1.0) * rates)
        direct = skip[:, cols]
        for b in range(blocks):
            here = slice(b * SUB, (b + 1) * SUB)
            gated = gext[(b + 1) * SUB : (b + 2) * SUB, cols]
            total = conv[here, cols] + jnp.sum(term, axis=0)
            queries[here, cols] = queries[here, cols] * (total + direct * gated)
            if b < blocks - 1:
                term = term * decay
    hyena[...] = queries[...].astype(jnp.bfloat16)
    hyena_copy.start()

    def product(rows_of, block, c, part):
        tile = weight[block, part * channels : (part + 1) * channels, c * piece : (c + 1) * piece]
        return jnp.dot(rows_of[...], tile, preferred_element_type=jnp.float32)

    loads[7].wait()
    for c in range(CHUNKS):
        own_part[c] = product(hyena, 0, c, 0)
    weight_copy(0).wait_recv()
    hyena_copy.wait_recv()
    for c in range(CHUNKS):
        cross_send[c] = (own_part[c] + product(twin_hyena, 0, c, 1)).astype(jnp.bfloat16)
        cross_copy(c).start()
    loads[8].wait()
    weight_copy(1).wait_recv()
    for c in range(CHUNKS):
        own_part[c] = product(hyena, 1, c, 0) + product(twin_hyena, 1, c, 1)
    def result_copy(c):
        cols = slice(c * piece, (c + 1) * piece)
        return pltpu.make_async_copy(result.at[c], out_hbm.at[:, cols], result_sem.at[c])

    for c in range(CHUNKS):
        cross_copy(c).wait_recv()
        total = own_part[c] + cross_recv[c].astype(jnp.float32)
        result[c] = total.astype(jnp.bfloat16)
        result_copy(c).start()

    for c in range(CHUNKS):
        cross_copy(c).wait_send()
    for i in range(2):
        weight_copy(i).wait_send()
    hyena_copy.wait_send()

    @pl.when(me < n_seq - 1)
    def _():
        for i in (1, 2, 0):
            halo_copy(i).wait_send()

    def sent(d, carry):
        state_copy(me, d).wait_send()
        head_copy(me, d).wait_send()
        return carry

    lax.fori_loop(me + 1, n_seq, sent, 0)
    for c in range(CHUNKS):
        result_copy(c).wait()


def solution(mesh):
    n_seq, n_tp = mesh.shape["seq"], mesh.shape["tp"]
    assert n_tp == 4

    def local(query_in, key_in, value_in, short_weight, residue, rate, skip, out_weight):
        rows, channels = query_in.shape
        order, n_taps = rate.shape[0], short_weight.shape[1]
        width = out_weight.shape[1] // n_tp
        piece = width // CHUNKS
        f32, bf16 = jnp.float32, jnp.bfloat16
        pieces = pltpu.VMEM((CHUNKS, rows, piece), bf16)
        return pl.pallas_call(
            functools.partial(kernel, n_seq, n_tp),
            out_shape=jax.ShapeDtypeStruct((rows, width), bf16),
            in_specs=[pl.BlockSpec(memory_space=pltpu.HBM)] * 8,
            out_specs=pl.BlockSpec(memory_space=pl.ANY),
            scratch_shapes=[
                pltpu.VMEM((3, rows, channels), bf16),
                pltpu.VMEM((3, n_taps, channels), f32),
                pltpu.VMEM((order, channels), f32),
                pltpu.VMEM((order, channels), f32),
                pltpu.VMEM((1, channels), f32),
                pltpu.VMEM((2, 2 * channels, width), bf16),
                pltpu.VMEM((3, EDGE, channels), bf16),
                pltpu.VMEM((3, rows + SUB, channels), f32),
                pltpu.VMEM((rows + SUB, channels), f32),
                pltpu.VMEM((rows + SUB, channels), f32),
                pltpu.VMEM((rows, channels), f32),
                pltpu.VMEM((n_seq, order, channels), bf16),
                pltpu.VMEM((order, channels), bf16),
                pltpu.VMEM((n_seq, SUB * channels // LANES, LANES), bf16),
                pltpu.VMEM((SUB * channels // LANES, LANES), bf16),
                pltpu.VMEM((rows, channels), f32),
                pltpu.VMEM((rows, channels), bf16),
                pltpu.VMEM((rows, channels), bf16),
                pieces,
                pieces,
                pieces,
                pltpu.VMEM((CHUNKS, rows, piece), f32),
                pltpu.SemaphoreType.DMA((9,)),
                pltpu.SemaphoreType.DMA((6,)),
                pltpu.SemaphoreType.DMA((n_seq,)),
                pltpu.SemaphoreType.DMA((n_seq,)),
                pltpu.SemaphoreType.DMA((n_seq,)),
                pltpu.SemaphoreType.DMA((n_seq,)),
                pltpu.SemaphoreType.DMA((6,)),
                pltpu.SemaphoreType.DMA((CHUNKS,)),
                pltpu.SemaphoreType.DMA((CHUNKS,)),
                pltpu.SemaphoreType.DMA((CHUNKS,)),
            ],
            compiler_params=pltpu.CompilerParams(
                collective_id=0, has_side_effects=True, vmem_limit_bytes=60 * 1024 * 1024
            ),
        )(
            query_in,
            key_in,
            value_in,
            short_weight,
            residue,
            rate,
            skip.reshape(1, channels),
            out_weight,
        )

    in_specs = (
        P("seq", "tp"),
        P("seq", "tp"),
        P("seq", "tp"),
        P(None, None, "tp"),
        P(None, "tp"),
        P(None, "tp"),
        P("tp"),
        P("tp", None),
    )
    return jax.shard_map(local, mesh=mesh, in_specs=in_specs, out_specs=P("seq", "tp"), check_vma=False)
```

```python
import functools

import jax
import jax.numpy as jnp
from jax import lax
from jax.experimental import pallas as pl
from jax.experimental.pallas import tpu as pltpu
from jax.sharding import PartitionSpec as P

MESH = pl.DeviceIdType.MESH
LANES = 128
SUB = 8
EDGE = 16
CHUNKS = 4


def one_minus_exp_neg(x):
    series = x * (1.0 - x * (1.0 / 2 - x * (1.0 / 6 - x * (1.0 / 24 - x * (1.0 / 120 - x * (1.0 / 720))))))
    return jnp.where(x < 0.2, series, 1.0 - jnp.exp(-x))


def kernel(
    n_seq,
    n_tp,
    query_hbm,
    key_hbm,
    value_hbm,
    taps_hbm,
    residue_hbm,
    rate_hbm,
    skip_hbm,
    weight_hbm,
    out_hbm,
    streams,
    taps,
    residue,
    rate,
    skip,
    weight,
    halo,
    extended,
    gext,
    filt,
    conv,
    states,
    own_state,
    queries,
    hyena,
    twin_hyena,
    result,
    cross_send,
    cross_recv,
    own_part,
    local_sem,
    halo_sem,
    state_send,
    state_recv,
    twin_sem,
    cross_out,
    cross_in,
    result_sem,
):
    rows, channels = query_hbm.shape
    order = rate_hbm.shape[0]
    n_taps = taps_hbm.shape[1]
    blocks = rows // SUB
    halves = channels // LANES
    width = out_hbm.shape[1]
    piece = width // CHUNKS
    me = lax.axis_index("seq")
    tp = lax.axis_index("tp")
    twin = tp + 1 - 2 * lax.rem(tp, 2)
    cross = lax.rem(tp + 2, n_tp)
    twin_cross = lax.rem(twin + 2, n_tp)

    def columns(block):
        return pl.ds(pl.multiple_of(block * width, width), width)

    own_rows, twin_rows = pl.ds(0, channels), pl.ds(channels, channels)
    loads = [
        pltpu.make_async_copy(src, dst, local_sem.at[i])
        for i, (src, dst) in enumerate(
            (
                (key_hbm, streams.at[1]),
                (value_hbm, streams.at[2]),
                (taps_hbm, taps),
                (rate_hbm, rate),
                (residue_hbm, residue),
                (query_hbm, streams.at[0]),
                (skip_hbm, skip),
                (weight_hbm.at[:, columns(cross)], weight.at[0, own_rows]),
                (weight_hbm.at[:, columns(tp)], weight.at[1, own_rows]),
            )
        )
    ]
    for load in loads:
        load.start()

    barrier = pltpu.get_barrier_semaphore()

    def greet(d, carry):
        pl.semaphore_signal(barrier, inc=1, device_id={"seq": d}, device_id_type=MESH)
        return carry

    lax.fori_loop(0, me, greet, 0)
    for partner in (twin, cross):
        pl.semaphore_signal(barrier, inc=1, device_id={"tp": partner}, device_id_type=MESH)

    step = lax.broadcasted_iota(jnp.int32, (order, SUB, LANES), 1).astype(jnp.float32)
    lanes = [slice(half * LANES, (half + 1) * LANES) for half in range(halves)]

    def cube(x):
        return jnp.broadcast_to(x[:, None, :], (order, SUB, LANES))

    def amplitude_of(cols):
        return residue[:, cols] * jnp.sqrt(one_minus_exp_neg(2.0 * rate[:, cols]))

    pl.semaphore_wait(barrier, n_seq - 1 - me + 2)

    def halo_copy(i):
        return pltpu.make_async_remote_copy(
            src_ref=(query_hbm, key_hbm, value_hbm)[i].at[pl.ds(rows - EDGE, EDGE)],
            dst_ref=halo.at[i],
            send_sem=halo_sem.at[i],
            recv_sem=halo_sem.at[3 + i],
            device_id={"seq": lax.rem(me + 1, n_seq)},
            device_id_type=MESH,
        )

    def state_copy(slot, d):
        return pltpu.make_async_remote_copy(
            src_ref=own_state,
            dst_ref=states.at[slot],
            send_sem=state_send.at[d],
            recv_sem=state_recv.at[slot],
            device_id={"seq": d},
            device_id_type=MESH,
        )

    def weight_copy(i):
        return pltpu.make_async_remote_copy(
            src_ref=weight_hbm.at[:, columns((twin_cross, twin)[i])],
            dst_ref=weight.at[i, twin_rows],
            send_sem=twin_sem.at[i],
            recv_sem=twin_sem.at[3 + i],
            device_id={"tp": twin},
            device_id_type=MESH,
        )

    hyena_copy = pltpu.make_async_remote_copy(
        src_ref=hyena,
        dst_ref=twin_hyena,
        send_sem=twin_sem.at[2],
        recv_sem=twin_sem.at[5],
        device_id={"tp": twin},
        device_id_type=MESH,
    )

    def cross_copy(c):
        return pltpu.make_async_remote_copy(
            src_ref=cross_send.at[c],
            dst_ref=cross_recv.at[c],
            send_sem=cross_out.at[c],
            recv_sem=cross_in.at[c],
            device_id={"tp": cross},
            device_id_type=MESH,
        )

    @pl.when(me < n_seq - 1)
    def _():
        for i in (1, 2, 0):
            halo_copy(i).start()

    def short_conv(i, first, count):
        total = jnp.zeros((count, channels), jnp.float32)
        for t in range(n_taps):
            begin = first + SUB - t
            total = total + taps[i, t : t + 1, :] * extended[i, begin : begin + count]
        return total

    for load in loads[:3]:
        load.wait()
    gext[0:SUB] = jnp.zeros((SUB, channels), jnp.float32)
    for i in (1, 2):
        extended[i, SUB:] = streams[i].astype(jnp.float32)
    gext[2 * SUB :] = short_conv(1, SUB, rows - SUB) * short_conv(2, SUB, rows - SUB)

    @pl.when(me == 0)
    def _():
        halo[...] = jnp.zeros_like(halo)

    @pl.when(me > 0)
    def _():
        for i in (1, 2, 0):
            halo_copy(i).wait_recv()

    for i in range(3):
        extended[i, 0:SUB] = halo[i].astype(jnp.float32)[EDGE - SUB :]
    gext[SUB : 2 * SUB] = short_conv(1, 0, SUB) * short_conv(2, 0, SUB)

    for load in loads[3:5]:
        load.wait()
    for cols in lanes:
        rates = cube(rate[:, cols])
        decay = jnp.exp(-float(SUB) * rates)
        total = jnp.broadcast_to(gext[SUB : 2 * SUB, cols][None], (order, SUB, LANES))
        for b in range(1, blocks):
            total = total * decay + gext[(b + 1) * SUB : (b + 2) * SUB, cols][None]
        total = total * jnp.exp((step - float(SUB - 1)) * rates)
        own_state[:, cols] = jnp.sum(total, axis=1).astype(jnp.bfloat16)

    def send_state(i, carry):
        state_copy(me, n_seq - 1 - i).start()
        return carry

    lax.fori_loop(0, n_seq - 1 - me, send_state, 0)
    for i in range(2):
        weight_copy(i).start()

    for cols in lanes:
        rates = cube(rate[:, cols])
        decay = jnp.exp(-float(SUB) * rates)
        term = cube(amplitude_of(cols)) * jnp.exp(-step * rates)
        for b in range(blocks):
            filt[b * SUB : (b + 1) * SUB, cols] = jnp.sum(term, axis=0)
            if b < blocks - 1:
                term = term * decay

    def local_conv(half, carry):
        cols = pl.ds(pl.multiple_of(half * LANES, LANES), LANES)
        total = jnp.zeros((rows, LANES), jnp.float32)
        for s in range(SUB):
            shifted = gext[SUB - s : SUB - s + rows, cols]
            for q in range(blocks):
                tap = filt[q * SUB + s : q * SUB + s + 1, cols]
                if q == 0:
                    total = total + tap * shifted
                else:
                    lower = total[q * SUB :] + tap * shifted[: rows - q * SUB]
                    total = jnp.concatenate([total[: q * SUB], lower], axis=0)
        conv[:, cols] = total
        return carry

    lax.fori_loop(0, halves, local_conv, 0)

    loads[5].wait()
    extended[0, SUB:] = streams[0].astype(jnp.float32)
    queries[...] = short_conv(0, 0, rows)

    loads[6].wait()
    spans = jnp.exp(-float(rows) * rate[...])

    def take_state(d, held):
        state_copy(d, d).wait_recv()
        return held * spans + states[d].astype(jnp.float32)

    held = lax.fori_loop(0, me, take_state, jnp.zeros((order, channels), jnp.float32))

    for cols in lanes:
        rates = cube(rate[:, cols])
        decay = jnp.exp(-float(SUB) * rates)
        term = cube(amplitude_of(cols) * held[:, cols]) * jnp.exp(-(step + 1.0) * rates)
        direct = skip[:, cols]
        for b in range(blocks):
            here = slice(b * SUB, (b + 1) * SUB)
            gated = gext[(b + 1) * SUB : (b + 2) * SUB, cols]
            total = conv[here, cols] + jnp.sum(term, axis=0)
            queries[here, cols] = queries[here, cols] * (total + direct * gated)
            if b < blocks - 1:
                term = term * decay
    hyena[...] = queries[...].astype(jnp.bfloat16)
    hyena_copy.start()

    def product(rows_of, block, c, part):
        tile = weight[block, part * channels : (part + 1) * channels, c * piece : (c + 1) * piece]
        return jnp.dot(rows_of[...], tile, preferred_element_type=jnp.float32)

    loads[7].wait()
    for c in range(CHUNKS):
        own_part[c] = product(hyena, 0, c, 0)
    weight_copy(0).wait_recv()
    hyena_copy.wait_recv()
    for c in range(CHUNKS):
        cross_send[c] = (own_part[c] + product(twin_hyena, 0, c, 1)).astype(jnp.bfloat16)
        cross_copy(c).start()
    loads[8].wait()
    weight_copy(1).wait_recv()
    for c in range(CHUNKS):
        own_part[c] = product(hyena, 1, c, 0) + product(twin_hyena, 1, c, 1)
    def result_copy(c):
        cols = slice(c * piece, (c + 1) * piece)
        return pltpu.make_async_copy(result.at[c], out_hbm.at[:, cols], result_sem.at[c])

    for c in range(CHUNKS):
        cross_copy(c).wait_recv()
        total = own_part[c] + cross_recv[c].astype(jnp.float32)
        result[c] = total.astype(jnp.bfloat16)
        result_copy(c).start()

    for c in range(CHUNKS):
        cross_copy(c).wait_send()
    for i in range(2):
        weight_copy(i).wait_send()
    hyena_copy.wait_send()

    @pl.when(me < n_seq - 1)
    def _():
        for i in (1, 2, 0):
            halo_copy(i).wait_send()

    def sent(d, carry):
        state_copy(me, d).wait_send()
        return carry

    lax.fori_loop(me + 1, n_seq, sent, 0)
    for c in range(CHUNKS):
        result_copy(c).wait()


def solution(mesh):
    n_seq, n_tp = mesh.shape["seq"], mesh.shape["tp"]
    assert n_tp == 4

    def local(query_in, key_in, value_in, short_weight, residue, rate, skip, out_weight):
        rows, channels = query_in.shape
        order, n_taps = rate.shape[0], short_weight.shape[1]
        width = out_weight.shape[1] // n_tp
        piece = width // CHUNKS
        f32, bf16 = jnp.float32, jnp.bfloat16
        pieces = pltpu.VMEM((CHUNKS, rows, piece), bf16)
        return pl.pallas_call(
            functools.partial(kernel, n_seq, n_tp),
            out_shape=jax.ShapeDtypeStruct((rows, width), bf16),
            in_specs=[pl.BlockSpec(memory_space=pltpu.HBM)] * 8,
            out_specs=pl.BlockSpec(memory_space=pl.ANY),
            scratch_shapes=[
                pltpu.VMEM((3, rows, channels), bf16),
                pltpu.VMEM((3, n_taps, channels), f32),
                pltpu.VMEM((order, channels), f32),
                pltpu.VMEM((order, channels), f32),
                pltpu.VMEM((1, channels), f32),
                pltpu.VMEM((2, 2 * channels, width), bf16),
                pltpu.VMEM((3, EDGE, channels), bf16),
                pltpu.VMEM((3, rows + SUB, channels), f32),
                pltpu.VMEM((rows + SUB, channels), f32),
                pltpu.VMEM((rows, channels), f32),
                pltpu.VMEM((rows, channels), f32),
                pltpu.VMEM((n_seq, order, channels), bf16),
                pltpu.VMEM((order, channels), bf16),
                pltpu.VMEM((rows, channels), f32),
                pltpu.VMEM((rows, channels), bf16),
                pltpu.VMEM((rows, channels), bf16),
                pieces,
                pieces,
                pieces,
                pltpu.VMEM((CHUNKS, rows, piece), f32),
                pltpu.SemaphoreType.DMA((9,)),
                pltpu.SemaphoreType.DMA((6,)),
                pltpu.SemaphoreType.DMA((n_seq,)),
                pltpu.SemaphoreType.DMA((n_seq,)),
                pltpu.SemaphoreType.DMA((6,)),
                pltpu.SemaphoreType.DMA((CHUNKS,)),
                pltpu.SemaphoreType.DMA((CHUNKS,)),
                pltpu.SemaphoreType.DMA((CHUNKS,)),
            ],
            compiler_params=pltpu.CompilerParams(
                collective_id=0, has_side_effects=True, vmem_limit_bytes=60 * 1024 * 1024
            ),
        )(
            query_in,
            key_in,
            value_in,
            short_weight,
            residue,
            rate,
            skip.reshape(1, channels),
            out_weight,
        )

    in_specs = (
        P("seq", "tp"),
        P("seq", "tp"),
        P("seq", "tp"),
        P(None, None, "tp"),
        P(None, "tp"),
        P(None, "tp"),
        P("tp"),
        P("tp", None),
    )
    return jax.shard_map(local, mesh=mesh, in_specs=in_specs, out_specs=P("seq", "tp"), check_vma=False)
```

```python
import functools

import jax
import jax.numpy as jnp
from jax import lax
from jax.experimental import pallas as pl
from jax.experimental.pallas import tpu as pltpu
from jax.sharding import PartitionSpec as P

MESH = pl.DeviceIdType.MESH
LANES = 128
SUB = 8
EDGE = 16
CHUNKS = 4


def one_minus_exp_neg(x):
    series = x * (1.0 - x * (1.0 / 2 - x * (1.0 / 6 - x * (1.0 / 24 - x * (1.0 / 120 - x * (1.0 / 720))))))
    return jnp.where(x < 0.2, series, 1.0 - jnp.exp(-x))


def kernel(
    n_seq,
    n_tp,
    query_hbm,
    key_hbm,
    value_hbm,
    taps_hbm,
    residue_hbm,
    rate_hbm,
    skip_hbm,
    weight_hbm,
    out_ref,
    streams,
    taps,
    residue,
    rate,
    skip,
    weight,
    halo,
    extended,
    gext,
    fext,
    conv,
    states,
    own_state,
    heads,
    own_head,
    queries,
    hyena,
    twin_hyena,
    cross_send,
    cross_recv,
    own_part,
    local_sem,
    halo_sem,
    state_send,
    state_recv,
    head_send,
    head_recv,
    twin_sem,
    cross_out,
    cross_in,
):
    rows, channels = query_hbm.shape
    order = rate_hbm.shape[0]
    n_taps = taps_hbm.shape[1]
    blocks = rows // SUB
    halves = channels // LANES
    width = out_ref.shape[1]
    piece = width // CHUNKS
    me = lax.axis_index("seq")
    tp = lax.axis_index("tp")
    twin = tp + 1 - 2 * lax.rem(tp, 2)
    cross = lax.rem(tp + 2, n_tp)
    twin_cross = lax.rem(twin + 2, n_tp)

    def columns(block):
        return pl.ds(pl.multiple_of(block * width, width), width)

    own_rows, twin_rows = pl.ds(0, channels), pl.ds(channels, channels)
    loads = [
        pltpu.make_async_copy(src, dst, local_sem.at[i])
        for i, (src, dst) in enumerate(
            (
                (rate_hbm, rate),
                (residue_hbm, residue),
                (key_hbm, streams.at[1]),
                (value_hbm, streams.at[2]),
                (taps_hbm, taps),
                (query_hbm, streams.at[0]),
                (skip_hbm, skip),
                (weight_hbm.at[:, columns(cross)], weight.at[0, own_rows]),
                (weight_hbm.at[:, columns(tp)], weight.at[1, own_rows]),
            )
        )
    ]
    for load in loads:
        load.start()

    barrier = pltpu.get_barrier_semaphore()

    def greet(d, carry):
        pl.semaphore_signal(barrier, inc=1, device_id={"seq": d}, device_id_type=MESH)
        return carry

    lax.fori_loop(0, me, greet, 0)
    for partner in (twin, cross):
        pl.semaphore_signal(barrier, inc=1, device_id={"tp": partner}, device_id_type=MESH)

    step = lax.broadcasted_iota(jnp.int32, (order, SUB, LANES), 1).astype(jnp.float32)
    lanes = [slice(half * LANES, (half + 1) * LANES) for half in range(halves)]

    def cube(x):
        return jnp.broadcast_to(x[:, None, :], (order, SUB, LANES))

    def amplitude_of(cols):
        return residue[:, cols] * jnp.sqrt(one_minus_exp_neg(2.0 * rate[:, cols]))

    for load in loads[:2]:
        load.wait()
    fext[0:SUB] = jnp.zeros((SUB, channels), jnp.float32)
    for cols in lanes:
        rates = cube(rate[:, cols])
        decay = jnp.exp(-float(SUB) * rates)
        term = cube(amplitude_of(cols)) * jnp.exp(-step * rates)
        for b in range(blocks):
            fext[(b + 1) * SUB : (b + 2) * SUB, cols] = jnp.sum(term, axis=0)
            if b < blocks - 1:
                term = term * decay

    for load in loads[2:6]:
        load.wait()

    def short_conv(i, first, count):
        total = jnp.zeros((count, channels), jnp.float32)
        for t in range(n_taps):
            begin = first + SUB - t
            total = total + taps[i, t : t + 1, :] * extended[i, begin : begin + count]
        return total

    for i in range(3):
        extended[i, SUB:] = streams[i].astype(jnp.float32)
    gext[0 : 2 * SUB] = jnp.zeros((2 * SUB, channels), jnp.float32)
    gext[2 * SUB :] = short_conv(1, SUB, rows - SUB) * short_conv(2, SUB, rows - SUB)

    for cols in lanes:
        rates = cube(rate[:, cols])
        decay = jnp.exp(-float(SUB) * rates)
        total = jnp.broadcast_to(gext[2 * SUB : 3 * SUB, cols][None], (order, SUB, LANES))
        for b in range(2, blocks):
            total = total * decay + gext[(b + 1) * SUB : (b + 2) * SUB, cols][None]
        total = total * jnp.exp((step - float(SUB - 1)) * rates)
        own_state[:, cols] = jnp.sum(total, axis=1).astype(jnp.bfloat16)

    pl.semaphore_wait(barrier, n_seq - 1 - me + 2)

    def halo_copy(i):
        return pltpu.make_async_remote_copy(
            src_ref=streams.at[i, pl.ds(rows - EDGE, EDGE)],
            dst_ref=halo.at[i],
            send_sem=halo_sem.at[i],
            recv_sem=halo_sem.at[3 + i],
            device_id={"seq": lax.rem(me + 1, n_seq)},
            device_id_type=MESH,
        )

    def state_copy(slot, d):
        return pltpu.make_async_remote_copy(
            src_ref=own_state,
            dst_ref=states.at[slot],
            send_sem=state_send.at[d],
            recv_sem=state_recv.at[slot],
            device_id={"seq": d},
            device_id_type=MESH,
        )

    def head_copy(slot, d):
        return pltpu.make_async_remote_copy(
            src_ref=own_head,
            dst_ref=heads.at[slot],
            send_sem=head_send.at[d],
            recv_sem=head_recv.at[slot],
            device_id={"seq": d},
            device_id_type=MESH,
        )

    def weight_copy(i):
        return pltpu.make_async_remote_copy(
            src_ref=weight_hbm.at[:, columns((twin_cross, twin)[i])],
            dst_ref=weight.at[i, twin_rows],
            send_sem=twin_sem.at[i],
            recv_sem=twin_sem.at[3 + i],
            device_id={"tp": twin},
            device_id_type=MESH,
        )

    hyena_copy = pltpu.make_async_remote_copy(
        src_ref=hyena,
        dst_ref=twin_hyena,
        send_sem=twin_sem.at[2],
        recv_sem=twin_sem.at[5],
        device_id={"tp": twin},
        device_id_type=MESH,
    )

    def cross_copy(c):
        return pltpu.make_async_remote_copy(
            src_ref=cross_send.at[c],
            dst_ref=cross_recv.at[c],
            send_sem=cross_out.at[c],
            recv_sem=cross_in.at[c],
            device_id={"tp": cross},
            device_id_type=MESH,
        )

    @pl.when(me < n_seq - 1)
    def _():
        for i in (1, 2, 0):
            halo_copy(i).start()

    def send_state(i, carry):
        state_copy(me, n_seq - 1 - i).start()
        return carry

    lax.fori_loop(0, n_seq - 1 - me, send_state, 0)
    for i in range(2):
        weight_copy(i).start()

    def local_conv(half, carry):
        cols = pl.ds(pl.multiple_of(half * LANES, LANES), LANES)
        total = jnp.zeros((rows, LANES), jnp.float32)
        for s in range(SUB):
            shifted = gext[SUB - s : SUB - s + rows, cols]
            for q in range(blocks):
                tap = fext[(q + 1) * SUB + s : (q + 1) * SUB + s + 1, cols]
                if q == 0:
                    total = total + tap * shifted
                else:
                    lower = total[q * SUB :] + tap * shifted[: rows - q * SUB]
                    total = jnp.concatenate([total[: q * SUB], lower], axis=0)
        conv[:, cols] = total
        return carry

    lax.fori_loop(0, halves, local_conv, 0)

    @pl.when(me == 0)
    def _():
        halo[...] = jnp.zeros_like(halo)

    @pl.when(me > 0)
    def _():
        for i in (1, 2, 0):
            halo_copy(i).wait_recv()

    for i in range(3):
        extended[i, 0:SUB] = halo[i].astype(jnp.float32)[EDGE - SUB :]
    head = short_conv(1, 0, SUB) * short_conv(2, 0, SUB)
    stacked = jnp.concatenate([head[:, cols] for cols in lanes], axis=0)
    own_head[...] = stacked.astype(jnp.bfloat16)
    gext[SUB : 2 * SUB] = head

    def send_head(i, carry):
        head_copy(me, n_seq - 1 - i).start()
        return carry

    lax.fori_loop(0, n_seq - 1 - me, send_head, 0)

    queries[...] = short_conv(0, 0, rows)
    for cols in lanes:
        total = conv[:, cols]
        for j in range(SUB):
            total = total + gext[SUB + j : SUB + j + 1, cols] * fext[SUB - j : SUB - j + rows, cols]
        conv[:, cols] = total

    loads[6].wait()
    spans = jnp.exp(-float(rows) * rate[...])
    wide = jnp.broadcast_to(spans[:, None, :], (order, SUB, channels))

    def take_state(d, carry):
        held, front = carry
        state_copy(d, d).wait_recv()
        head_copy(d, d).wait_recv()
        stacked = heads[d].astype(jnp.float32)
        head = jnp.concatenate(
            [stacked[half * SUB : (half + 1) * SUB] for half in range(halves)], axis=1
        )
        return held * spans + states[d].astype(jnp.float32), front * wide + head[None]

    held, front = lax.fori_loop(
        0,
        me,
        take_state,
        (
            jnp.zeros((order, channels), jnp.float32),
            jnp.zeros((order, SUB, channels), jnp.float32),
        ),
    )

    for cols in lanes:
        rates = cube(rate[:, cols])
        decay = jnp.exp(-float(SUB) * rates)
        ahead = jnp.exp((step - float(rows - 1)) * rates) * front[:, :, cols]
        carried = amplitude_of(cols) * (held[:, cols] + jnp.sum(ahead, axis=1))
        term = cube(carried) * jnp.exp(-(step + 1.0) * rates)
        direct = skip[:, cols]
        for b in range(blocks):
            here = slice(b * SUB, (b + 1) * SUB)
            gated = gext[(b + 1) * SUB : (b + 2) * SUB, cols]
            total = conv[here, cols] + jnp.sum(term, axis=0)
            queries[here, cols] = queries[here, cols] * (total + direct * gated)
            if b < blocks - 1:
                term = term * decay
    hyena[...] = queries[...].astype(jnp.bfloat16)
    hyena_copy.start()

    def product(rows_of, block, c, part):
        tile = weight[block, part * channels : (part + 1) * channels, c * piece : (c + 1) * piece]
        return jnp.dot(rows_of[...], tile, preferred_element_type=jnp.float32)

    loads[7].wait()
    for c in range(CHUNKS):
        own_part[c] = product(hyena, 0, c, 0)
    weight_copy(0).wait_recv()
    hyena_copy.wait_recv()
    for c in range(CHUNKS):
        cross_send[c] = (own_part[c] + product(twin_hyena, 0, c, 1)).astype(jnp.bfloat16)
        cross_copy(c).start()
    loads[8].wait()
    weight_copy(1).wait_recv()
    for c in range(CHUNKS):
        own_part[c] = product(hyena, 1, c, 0) + product(twin_hyena, 1, c, 1)
    for c in range(CHUNKS):
        cross_copy(c).wait_recv()
        total = own_part[c] + cross_recv[c].astype(jnp.float32)
        out_ref[:, c * piece : (c + 1) * piece] = total.astype(out_ref.dtype)

    for c in range(CHUNKS):
        cross_copy(c).wait_send()
    for i in range(2):
        weight_copy(i).wait_send()
    hyena_copy.wait_send()

    @pl.when(me < n_seq - 1)
    def _():
        for i in (1, 2, 0):
            halo_copy(i).wait_send()

    def sent(d, carry):
        state_copy(me, d).wait_send()
        head_copy(me, d).wait_send()
        return carry

    lax.fori_loop(me + 1, n_seq, sent, 0)


def solution(mesh):
    n_seq, n_tp = mesh.shape["seq"], mesh.shape["tp"]
    assert n_tp == 4

    def local(query_in, key_in, value_in, short_weight, residue, rate, skip, out_weight):
        rows, channels = query_in.shape
        order, n_taps = rate.shape[0], short_weight.shape[1]
        width = out_weight.shape[1] // n_tp
        piece = width // CHUNKS
        f32, bf16 = jnp.float32, jnp.bfloat16
        pieces = pltpu.VMEM((CHUNKS, rows, piece), bf16)
        operands = (
            query_in,
            key_in,
            value_in,
            short_weight,
            residue,
            rate,
            skip.reshape(1, channels),
            out_weight,
        )
        return pl.pallas_call(
            functools.partial(kernel, n_seq, n_tp),
            out_shape=jax.ShapeDtypeStruct((rows, width), bf16),
            in_specs=[pl.BlockSpec(memory_space=pltpu.HBM)] * 8,
            out_specs=pl.BlockSpec(memory_space=pltpu.VMEM),
            scratch_shapes=[
                pltpu.VMEM((3, rows, channels), bf16),
                pltpu.VMEM((3, n_taps, channels), f32),
                pltpu.VMEM((order, channels), f32),
                pltpu.VMEM((order, channels), f32),
                pltpu.VMEM((1, channels), f32),
                pltpu.VMEM((2, 2 * channels, width), bf16),
                pltpu.VMEM((3, EDGE, channels), bf16),
                pltpu.VMEM((3, rows + SUB, channels), f32),
                pltpu.VMEM((rows + SUB, channels), f32),
                pltpu.VMEM((rows + SUB, channels), f32),
                pltpu.VMEM((rows, channels), f32),
                pltpu.VMEM((n_seq, order, channels), bf16),
                pltpu.VMEM((order, channels), bf16),
                pltpu.VMEM((n_seq, SUB * channels // LANES, LANES), bf16),
                pltpu.VMEM((SUB * channels // LANES, LANES), bf16),
                pltpu.VMEM((rows, channels), f32),
                pltpu.VMEM((rows, channels), bf16),
                pltpu.VMEM((rows, channels), bf16),
                pieces,
                pieces,
                pltpu.VMEM((CHUNKS, rows, piece), f32),
                pltpu.SemaphoreType.DMA((9,)),
                pltpu.SemaphoreType.DMA((6,)),
                pltpu.SemaphoreType.DMA((n_seq,)),
                pltpu.SemaphoreType.DMA((n_seq,)),
                pltpu.SemaphoreType.DMA((n_seq,)),
                pltpu.SemaphoreType.DMA((n_seq,)),
                pltpu.SemaphoreType.DMA((6,)),
                pltpu.SemaphoreType.DMA((CHUNKS,)),
                pltpu.SemaphoreType.DMA((CHUNKS,)),
            ],
            compiler_params=pltpu.CompilerParams(
                collective_id=0, has_side_effects=True, vmem_limit_bytes=40 * 1024 * 1024
            ),
        )(
            *[pltpu.with_memory_space_constraint(x, pltpu.HBM) for x in operands]
        )

    in_specs = (
        P("seq", "tp"),
        P("seq", "tp"),
        P("seq", "tp"),
        P(None, None, "tp"),
        P(None, "tp"),
        P(None, "tp"),
        P("tp"),
        P("tp", None),
    )
    return jax.shard_map(local, mesh=mesh, in_specs=in_specs, out_specs=P("seq", "tp"), check_vma=False)
```

```python
import functools

import jax
import jax.numpy as jnp
from jax import lax
from jax.experimental import pallas as pl
from jax.experimental.pallas import tpu as pltpu
from jax.sharding import PartitionSpec as P

MESH = pl.DeviceIdType.MESH
LANES = 128
SUB = 8
EDGE = 16
CHUNKS = 4
EARLY = 1


def one_minus_exp_neg(x):
    series = x * (1.0 - x * (1.0 / 2 - x * (1.0 / 6 - x * (1.0 / 24 - x * (1.0 / 120 - x * (1.0 / 720))))))
    return jnp.where(x < 0.2, series, 1.0 - jnp.exp(-x))


def kernel(
    n_seq,
    n_tp,
    query_hbm,
    key_hbm,
    value_hbm,
    taps_hbm,
    residue_hbm,
    rate_hbm,
    skip_hbm,
    weight_hbm,
    out_ref,
    streams,
    taps,
    residue,
    rate,
    skip,
    weight,
    cross_weight,
    far_weight,
    halo,
    extended,
    gext,
    fext,
    conv,
    states,
    own_state,
    heads,
    own_head,
    queries,
    hyena,
    twin_hyena,
    cross_hyena,
    far_hyena,
    cross_send,
    cross_recv,
    own_part,
    local_sem,
    halo_sem,
    state_send,
    state_recv,
    head_send,
    head_recv,
    tp_out,
    tp_in,
    cross_out,
    cross_in,
):
    rows, channels = query_hbm.shape
    order = rate_hbm.shape[0]
    n_taps = taps_hbm.shape[1]
    blocks = rows // SUB
    halves = channels // LANES
    width = out_ref.shape[1]
    piece = width // CHUNKS
    me = lax.axis_index("seq")
    tp = lax.axis_index("tp")
    twin = tp + 1 - 2 * lax.rem(tp, 2)
    cross = lax.rem(tp + 2, n_tp)
    twin_cross = lax.rem(twin + 2, n_tp)

    early = EARLY * piece

    def columns(block, first=0, count=width):
        return pl.ds(pl.multiple_of(block * width + first, piece), count)

    own_rows, twin_rows = pl.ds(0, channels), pl.ds(channels, channels)
    loads = [
        pltpu.make_async_copy(src, dst, local_sem.at[i])
        for i, (src, dst) in enumerate(
            (
                (rate_hbm, rate),
                (residue_hbm, residue),
                (key_hbm, streams.at[1]),
                (value_hbm, streams.at[2]),
                (taps_hbm, taps),
                (query_hbm, streams.at[0]),
                (skip_hbm, skip),
                (weight_hbm.at[:, columns(cross, early, width - early)], cross_weight.at[own_rows]),
                (weight_hbm.at[:, columns(tp)], weight.at[own_rows]),
            )
        )
    ]
    for load in loads:
        load.start()

    barrier = pltpu.get_barrier_semaphore()

    def greet(d, carry):
        pl.semaphore_signal(barrier, inc=1, device_id={"seq": d}, device_id_type=MESH)
        return carry

    lax.fori_loop(0, me, greet, 0)
    for partner in (twin, cross, twin_cross):
        pl.semaphore_signal(barrier, inc=1, device_id={"tp": partner}, device_id_type=MESH)

    step = lax.broadcasted_iota(jnp.int32, (order, SUB, LANES), 1).astype(jnp.float32)
    lanes = [slice(half * LANES, (half + 1) * LANES) for half in range(halves)]

    def cube(x):
        return jnp.broadcast_to(x[:, None, :], (order, SUB, LANES))

    def amplitude_of(cols):
        return residue[:, cols] * jnp.sqrt(one_minus_exp_neg(2.0 * rate[:, cols]))

    for load in loads[:2]:
        load.wait()
    fext[0:SUB] = jnp.zeros((SUB, channels), jnp.float32)
    for cols in lanes:
        rates = cube(rate[:, cols])
        decay = jnp.exp(-float(SUB) * rates)
        term = cube(amplitude_of(cols)) * jnp.exp(-step * rates)
        for b in range(blocks):
            fext[(b + 1) * SUB : (b + 2) * SUB, cols] = jnp.sum(term, axis=0)
            if b < blocks - 1:
                term = term * decay

    for load in loads[2:6]:
        load.wait()

    def short_conv(i, first, count):
        total = jnp.zeros((count, channels), jnp.float32)
        for t in range(n_taps):
            begin = first + SUB - t
            total = total + taps[i, t : t + 1, :] * extended[i, begin : begin + count]
        return total

    for i in range(3):
        extended[i, SUB:] = streams[i].astype(jnp.float32)
    gext[0 : 2 * SUB] = jnp.zeros((2 * SUB, channels), jnp.float32)
    gext[2 * SUB :] = short_conv(1, SUB, rows - SUB) * short_conv(2, SUB, rows - SUB)

    for cols in lanes:
        rates = cube(rate[:, cols])
        decay = jnp.exp(-float(SUB) * rates)
        total = jnp.broadcast_to(gext[2 * SUB : 3 * SUB, cols][None], (order, SUB, LANES))
        for b in range(2, blocks):
            total = total * decay + gext[(b + 1) * SUB : (b + 2) * SUB, cols][None]
        total = total * jnp.exp((step - float(SUB - 1)) * rates)
        own_state[:, cols] = jnp.sum(total, axis=1).astype(jnp.bfloat16)

    pl.semaphore_wait(barrier, n_seq - 1 - me + 3)

    def halo_copy(i):
        return pltpu.make_async_remote_copy(
            src_ref=streams.at[i, pl.ds(rows - EDGE, EDGE)],
            dst_ref=halo.at[i],
            send_sem=halo_sem.at[i],
            recv_sem=halo_sem.at[3 + i],
            device_id={"seq": lax.rem(me + 1, n_seq)},
            device_id_type=MESH,
        )

    def state_copy(slot, d):
        return pltpu.make_async_remote_copy(
            src_ref=own_state,
            dst_ref=states.at[slot],
            send_sem=state_send.at[d],
            recv_sem=state_recv.at[slot],
            device_id={"seq": d},
            device_id_type=MESH,
        )

    def head_copy(slot, d):
        return pltpu.make_async_remote_copy(
            src_ref=own_head,
            dst_ref=heads.at[slot],
            send_sem=head_send.at[d],
            recv_sem=head_recv.at[slot],
            device_id={"seq": d},
            device_id_type=MESH,
        )

    def tp_copy(i, src, dst, target):
        return pltpu.make_async_remote_copy(
            src_ref=src,
            dst_ref=dst,
            send_sem=tp_out.at[i],
            recv_sem=tp_in.at[i],
            device_id={"tp": target},
            device_id_type=MESH,
        )

    weight_copies = (
        tp_copy(
            0,
            weight_hbm.at[:, columns(twin_cross, early, width - early)],
            cross_weight.at[twin_rows],
            twin,
        ),
        tp_copy(1, weight_hbm.at[:, columns(twin)], weight.at[twin_rows], twin),
        tp_copy(2, weight_hbm.at[:, columns(cross, 0, early)], far_weight.at[own_rows], cross),
        tp_copy(
            3,
            weight_hbm.at[:, columns(twin_cross, 0, early)],
            far_weight.at[twin_rows],
            twin_cross,
        ),
    )
    hyena_cross = tp_copy(4, hyena, cross_hyena, cross)
    hyena_twin = tp_copy(5, hyena, twin_hyena, twin)
    hyena_far = tp_copy(6, cross_hyena, far_hyena, twin)

    def cross_copy(c):
        return pltpu.make_async_remote_copy(
            src_ref=cross_send.at[c],
            dst_ref=cross_recv.at[c],
            send_sem=cross_out.at[c],
            recv_sem=cross_in.at[c],
            device_id={"tp": cross},
            device_id_type=MESH,
        )

    @pl.when(me < n_seq - 1)
    def _():
        for i in (1, 2, 0):
            halo_copy(i).start()

    def send_state(i, carry):
        state_copy(me, n_seq - 1 - i).start()
        return carry

    lax.fori_loop(0, n_seq - 1 - me, send_state, 0)
    for copy in weight_copies[2:]:
        copy.start()

    def local_conv(half, carry):
        cols = pl.ds(pl.multiple_of(half * LANES, LANES), LANES)
        total = jnp.zeros((rows, LANES), jnp.float32)
        for s in range(SUB):
            shifted = gext[SUB - s : SUB - s + rows, cols]
            for q in range(blocks):
                tap = fext[(q + 1) * SUB + s : (q + 1) * SUB + s + 1, cols]
                if q == 0:
                    total = total + tap * shifted
                else:
                    lower = total[q * SUB :] + tap * shifted[: rows - q * SUB]
                    total = jnp.concatenate([total[: q * SUB], lower], axis=0)
        conv[:, cols] = total
        return carry

    lax.fori_loop(0, halves, local_conv, 0)

    @pl.when(me == 0)
    def _():
        halo[...] = jnp.zeros_like(halo)

    @pl.when(me > 0)
    def _():
        for i in (1, 2, 0):
            halo_copy(i).wait_recv()

    for i in range(3):
        extended[i, 0:SUB] = halo[i].astype(jnp.float32)[EDGE - SUB :]
    head = short_conv(1, 0, SUB) * short_conv(2, 0, SUB)
    stacked = jnp.concatenate([head[:, cols] for cols in lanes], axis=0)
    own_head[...] = stacked.astype(jnp.bfloat16)
    gext[SUB : 2 * SUB] = head

    def send_head(i, carry):
        head_copy(me, n_seq - 1 - i).start()
        return carry

    lax.fori_loop(0, n_seq - 1 - me, send_head, 0)
    for copy in weight_copies[:2]:
        copy.start()

    queries[...] = short_conv(0, 0, rows)
    for cols in lanes:
        total = conv[:, cols]
        for j in range(SUB):
            total = total + gext[SUB + j : SUB + j + 1, cols] * fext[SUB - j : SUB - j + rows, cols]
        conv[:, cols] = total

    loads[6].wait()
    spans = jnp.exp(-float(rows) * rate[...])
    wide = jnp.broadcast_to(spans[:, None, :], (order, SUB, channels))

    def take_state(d, carry):
        held, front = carry
        state_copy(d, d).wait_recv()
        head_copy(d, d).wait_recv()
        stacked = heads[d].astype(jnp.float32)
        head = jnp.concatenate(
            [stacked[half * SUB : (half + 1) * SUB] for half in range(halves)], axis=1
        )
        return held * spans + states[d].astype(jnp.float32), front * wide + head[None]

    held, front = lax.fori_loop(
        0,
        me,
        take_state,
        (
            jnp.zeros((order, channels), jnp.float32),
            jnp.zeros((order, SUB, channels), jnp.float32),
        ),
    )

    for cols in lanes:
        rates = cube(rate[:, cols])
        decay = jnp.exp(-float(SUB) * rates)
        ahead = jnp.exp((step - float(rows - 1)) * rates) * front[:, :, cols]
        carried = amplitude_of(cols) * (held[:, cols] + jnp.sum(ahead, axis=1))
        term = cube(carried) * jnp.exp(-(step + 1.0) * rates)
        direct = skip[:, cols]
        for b in range(blocks):
            here = slice(b * SUB, (b + 1) * SUB)
            gated = gext[(b + 1) * SUB : (b + 2) * SUB, cols]
            total = conv[here, cols] + jnp.sum(term, axis=0)
            queries[here, cols] = queries[here, cols] * (total + direct * gated)
            if b < blocks - 1:
                term = term * decay
    hyena[...] = queries[...].astype(jnp.bfloat16)
    hyena_cross.start()
    hyena_twin.start()

    def product(rows_of, matrix, part, c):
        tile = matrix[part * channels : (part + 1) * channels, c * piece : (c + 1) * piece]
        return jnp.dot(rows_of[...], tile, preferred_element_type=jnp.float32)

    late = range(CHUNKS - EARLY)
    loads[7].wait()
    for c in late:
        own_part[c] = product(hyena, cross_weight, 0, c)
    weight_copies[0].wait_recv()
    hyena_twin.wait_recv()
    for c in late:
        cross_send[c] = (own_part[c] + product(twin_hyena, cross_weight, 1, c)).astype(jnp.bfloat16)
        cross_copy(c).start()
    hyena_cross.wait_recv()
    hyena_far.start()
    loads[8].wait()
    weight_copies[1].wait_recv()
    for c in range(CHUNKS):
        own_part[c] = product(hyena, weight, 0, c) + product(twin_hyena, weight, 1, c)
    weight_copies[2].wait_recv()
    for c in range(EARLY):
        own_part[c] = own_part[c] + product(cross_hyena, far_weight, 0, c)
    hyena_far.wait_recv()
    weight_copies[3].wait_recv()
    for c in range(EARLY):
        total = own_part[c] + product(far_hyena, far_weight, 1, c)
        out_ref[:, c * piece : (c + 1) * piece] = total.astype(out_ref.dtype)
    for c in late:
        cross_copy(c).wait_recv()
        total = own_part[EARLY + c] + cross_recv[c].astype(jnp.float32)
        out_ref[:, early + c * piece : early + (c + 1) * piece] = total.astype(out_ref.dtype)

    for c in late:
        cross_copy(c).wait_send()
    for copy in weight_copies + (hyena_cross, hyena_twin, hyena_far):
        copy.wait_send()

    @pl.when(me < n_seq - 1)
    def _():
        for i in (1, 2, 0):
            halo_copy(i).wait_send()

    def sent(d, carry):
        state_copy(me, d).wait_send()
        head_copy(me, d).wait_send()
        return carry

    lax.fori_loop(me + 1, n_seq, sent, 0)


def solution(mesh):
    n_seq, n_tp = mesh.shape["seq"], mesh.shape["tp"]
    assert n_tp == 4

    def local(query_in, key_in, value_in, short_weight, residue, rate, skip, out_weight):
        rows, channels = query_in.shape
        order, n_taps = rate.shape[0], short_weight.shape[1]
        width = out_weight.shape[1] // n_tp
        piece = width // CHUNKS
        f32, bf16 = jnp.float32, jnp.bfloat16
        pieces = pltpu.VMEM((CHUNKS - EARLY, rows, piece), bf16)
        operands = (
            query_in,
            key_in,
            value_in,
            short_weight,
            residue,
            rate,
            skip.reshape(1, channels),
            out_weight,
        )
        return pl.pallas_call(
            functools.partial(kernel, n_seq, n_tp),
            out_shape=jax.ShapeDtypeStruct((rows, width), bf16),
            in_specs=[pl.BlockSpec(memory_space=pltpu.HBM)] * 8,
            out_specs=pl.BlockSpec(memory_space=pltpu.VMEM),
            scratch_shapes=[
                pltpu.VMEM((3, rows, channels), bf16),
                pltpu.VMEM((3, n_taps, channels), f32),
                pltpu.VMEM((order, channels), f32),
                pltpu.VMEM((order, channels), f32),
                pltpu.VMEM((1, channels), f32),
                pltpu.VMEM((2 * channels, width), bf16),
                pltpu.VMEM((2 * channels, width - EARLY * piece), bf16),
                pltpu.VMEM((2 * channels, EARLY * piece), bf16),
                pltpu.VMEM((3, EDGE, channels), bf16),
                pltpu.VMEM((3, rows + SUB, channels), f32),
                pltpu.VMEM((rows + SUB, channels), f32),
                pltpu.VMEM((rows + SUB, channels), f32),
                pltpu.VMEM((rows, channels), f32),
                pltpu.VMEM((n_seq, order, channels), bf16),
                pltpu.VMEM((order, channels), bf16),
                pltpu.VMEM((n_seq, SUB * channels // LANES, LANES), bf16),
                pltpu.VMEM((SUB * channels // LANES, LANES), bf16),
                pltpu.VMEM((rows, channels), f32),
                pltpu.VMEM((rows, channels), bf16),
                pltpu.VMEM((rows, channels), bf16),
                pltpu.VMEM((rows, channels), bf16),
                pltpu.VMEM((rows, channels), bf16),
                pieces,
                pieces,
                pltpu.VMEM((CHUNKS, rows, piece), f32),
                pltpu.SemaphoreType.DMA((9,)),
                pltpu.SemaphoreType.DMA((6,)),
                pltpu.SemaphoreType.DMA((n_seq,)),
                pltpu.SemaphoreType.DMA((n_seq,)),
                pltpu.SemaphoreType.DMA((n_seq,)),
                pltpu.SemaphoreType.DMA((n_seq,)),
                pltpu.SemaphoreType.DMA((7,)),
                pltpu.SemaphoreType.DMA((7,)),
                pltpu.SemaphoreType.DMA((CHUNKS - EARLY,)),
                pltpu.SemaphoreType.DMA((CHUNKS - EARLY,)),
            ],
            compiler_params=pltpu.CompilerParams(
                collective_id=0, has_side_effects=True, vmem_limit_bytes=40 * 1024 * 1024
            ),
        )(
            *[pltpu.with_memory_space_constraint(x, pltpu.HBM) for x in operands]
        )

    in_specs = (
        P("seq", "tp"),
        P("seq", "tp"),
        P("seq", "tp"),
        P(None, None, "tp"),
        P(None, "tp"),
        P(None, "tp"),
        P("tp"),
        P("tp", None),
    )
    return jax.shard_map(local, mesh=mesh, in_specs=in_specs, out_specs=P("seq", "tp"), check_vma=False)
```

```python
import functools

import jax
import jax.numpy as jnp
from jax import lax
from jax.experimental import pallas as pl
from jax.experimental.pallas import tpu as pltpu
from jax.sharding import PartitionSpec as P

MESH = pl.DeviceIdType.MESH
LANES = 128
SUB = 8
EDGE = 16
CHUNKS = 4
EARLY = 1


def one_minus_exp_neg(x):
    series = x * (1.0 - x * (1.0 / 2 - x * (1.0 / 6 - x * (1.0 / 24 - x * (1.0 / 120 - x * (1.0 / 720))))))
    return jnp.where(x < 0.2, series, 1.0 - jnp.exp(-x))


def kernel(
    n_seq,
    n_tp,
    query_hbm,
    key_hbm,
    value_hbm,
    taps_hbm,
    residue_hbm,
    rate_hbm,
    skip_hbm,
    weight_hbm,
    out_ref,
    streams,
    taps,
    residue,
    rate,
    skip,
    weight,
    cross_weight,
    far_weight,
    halo,
    extended,
    gext,
    fext,
    conv,
    states,
    own_state,
    heads,
    own_head,
    queries,
    hyena,
    twin_hyena,
    cross_hyena,
    far_hyena,
    cross_send,
    cross_recv,
    own_part,
    local_sem,
    halo_sem,
    state_send,
    state_recv,
    head_send,
    head_recv,
    tp_out,
    tp_in,
    cross_out,
    cross_in,
):
    rows, channels = query_hbm.shape
    order = rate_hbm.shape[0]
    n_taps = taps_hbm.shape[1]
    blocks = rows // SUB
    halves = channels // LANES
    width = out_ref.shape[1]
    piece = width // CHUNKS
    me = lax.axis_index("seq")
    tp = lax.axis_index("tp")
    twin = tp + 1 - 2 * lax.rem(tp, 2)
    cross = lax.rem(tp + 2, n_tp)
    twin_cross = lax.rem(twin + 2, n_tp)

    early = EARLY * piece

    def columns(block, first=0, count=width):
        return pl.ds(pl.multiple_of(block * width + first, piece), count)

    own_rows, twin_rows = pl.ds(0, channels), pl.ds(channels, channels)
    loads = [
        pltpu.make_async_copy(src, dst, local_sem.at[i])
        for i, (src, dst) in enumerate(
            (
                (rate_hbm, rate),
                (residue_hbm, residue),
                (key_hbm, streams.at[1]),
                (value_hbm, streams.at[2]),
                (taps_hbm, taps),
                (query_hbm, streams.at[0]),
                (skip_hbm, skip),
                (weight_hbm.at[:, columns(cross)], cross_weight.at[own_rows]),
                (weight_hbm.at[:, columns(tp)], weight.at[own_rows]),
            )
        )
    ]
    for load in loads:
        load.start()

    barrier = pltpu.get_barrier_semaphore()

    def greet(d, carry):
        pl.semaphore_signal(barrier, inc=1, device_id={"seq": d}, device_id_type=MESH)
        return carry

    lax.fori_loop(0, me, greet, 0)
    for partner in (twin, cross, twin_cross):
        pl.semaphore_signal(barrier, inc=1, device_id={"tp": partner}, device_id_type=MESH)

    step = lax.broadcasted_iota(jnp.int32, (order, SUB, LANES), 1).astype(jnp.float32)
    lanes = [slice(half * LANES, (half + 1) * LANES) for half in range(halves)]

    def cube(x):
        return jnp.broadcast_to(x[:, None, :], (order, SUB, LANES))

    def amplitude_of(cols):
        return residue[:, cols] * jnp.sqrt(one_minus_exp_neg(2.0 * rate[:, cols]))

    for load in loads[:2]:
        load.wait()
    fext[0:SUB] = jnp.zeros((SUB, channels), jnp.float32)
    for cols in lanes:
        rates = cube(rate[:, cols])
        decay = jnp.exp(-float(SUB) * rates)
        term = cube(amplitude_of(cols)) * jnp.exp(-step * rates)
        for b in range(blocks):
            fext[(b + 1) * SUB : (b + 2) * SUB, cols] = jnp.sum(term, axis=0)
            if b < blocks - 1:
                term = term * decay

    for load in loads[2:6]:
        load.wait()

    def short_conv(i, first, count):
        total = jnp.zeros((count, channels), jnp.float32)
        for t in range(n_taps):
            begin = first + SUB - t
            total = total + taps[i, t : t + 1, :] * extended[i, begin : begin + count]
        return total

    for i in range(3):
        extended[i, SUB:] = streams[i].astype(jnp.float32)
    gext[0 : 2 * SUB] = jnp.zeros((2 * SUB, channels), jnp.float32)
    gext[2 * SUB :] = short_conv(1, SUB, rows - SUB) * short_conv(2, SUB, rows - SUB)

    for cols in lanes:
        rates = cube(rate[:, cols])
        decay = jnp.exp(-float(SUB) * rates)
        total = jnp.broadcast_to(gext[2 * SUB : 3 * SUB, cols][None], (order, SUB, LANES))
        for b in range(2, blocks):
            total = total * decay + gext[(b + 1) * SUB : (b + 2) * SUB, cols][None]
        total = total * jnp.exp((step - float(SUB - 1)) * rates)
        own_state[:, cols] = jnp.sum(total, axis=1).astype(jnp.bfloat16)

    pl.semaphore_wait(barrier, n_seq - 1 - me + 3)

    def halo_copy(i):
        return pltpu.make_async_remote_copy(
            src_ref=streams.at[i, pl.ds(rows - EDGE, EDGE)],
            dst_ref=halo.at[i],
            send_sem=halo_sem.at[i],
            recv_sem=halo_sem.at[3 + i],
            device_id={"seq": lax.rem(me + 1, n_seq)},
            device_id_type=MESH,
        )

    def state_copy(slot, d):
        return pltpu.make_async_remote_copy(
            src_ref=own_state,
            dst_ref=states.at[slot],
            send_sem=state_send.at[d],
            recv_sem=state_recv.at[slot],
            device_id={"seq": d},
            device_id_type=MESH,
        )

    def head_copy(slot, d):
        return pltpu.make_async_remote_copy(
            src_ref=own_head,
            dst_ref=heads.at[slot],
            send_sem=head_send.at[d],
            recv_sem=head_recv.at[slot],
            device_id={"seq": d},
            device_id_type=MESH,
        )

    def tp_copy(i, src, dst, target):
        return pltpu.make_async_remote_copy(
            src_ref=src,
            dst_ref=dst,
            send_sem=tp_out.at[i],
            recv_sem=tp_in.at[i],
            device_id={"tp": target},
            device_id_type=MESH,
        )

    weight_copies = (
        tp_copy(
            0,
            weight_hbm.at[:, columns(twin_cross)],
            cross_weight.at[twin_rows],
            twin,
        ),
        tp_copy(1, weight_hbm.at[:, columns(twin)], weight.at[twin_rows], twin),
        tp_copy(2, weight_hbm.at[:, columns(cross, 0, early)], far_weight.at[own_rows], cross),
        tp_copy(
            3,
            weight_hbm.at[:, columns(twin_cross, 0, early)],
            far_weight.at[twin_rows],
            twin_cross,
        ),
    )
    hyena_cross = tp_copy(4, hyena, cross_hyena, cross)
    hyena_twin = tp_copy(5, hyena, twin_hyena, twin)
    hyena_far = tp_copy(6, cross_hyena, far_hyena, twin)

    def cross_copy(c):
        return pltpu.make_async_remote_copy(
            src_ref=cross_send.at[c],
            dst_ref=cross_recv.at[c],
            send_sem=cross_out.at[c],
            recv_sem=cross_in.at[c],
            device_id={"tp": cross},
            device_id_type=MESH,
        )

    @pl.when(me < n_seq - 1)
    def _():
        for i in (1, 2, 0):
            halo_copy(i).start()

    def send_state(i, carry):
        state_copy(me, n_seq - 1 - i).start()
        return carry

    lax.fori_loop(0, n_seq - 1 - me, send_state, 0)
    @pl.when(me > 0)
    def _():
        for copy in weight_copies[2:]:
            copy.start()


    def local_conv(half, carry):
        cols = pl.ds(pl.multiple_of(half * LANES, LANES), LANES)
        total = jnp.zeros((rows, LANES), jnp.float32)
        for s in range(SUB):
            shifted = gext[SUB - s : SUB - s + rows, cols]
            for q in range(blocks):
                tap = fext[(q + 1) * SUB + s : (q + 1) * SUB + s + 1, cols]
                if q == 0:
                    total = total + tap * shifted
                else:
                    lower = total[q * SUB :] + tap * shifted[: rows - q * SUB]
                    total = jnp.concatenate([total[: q * SUB], lower], axis=0)
        conv[:, cols] = total
        return carry

    lax.fori_loop(0, halves, local_conv, 0)

    @pl.when(me == 0)
    def _():
        halo[...] = jnp.zeros_like(halo)

    @pl.when(me > 0)
    def _():
        for i in (1, 2, 0):
            halo_copy(i).wait_recv()

    for i in range(3):
        extended[i, 0:SUB] = halo[i].astype(jnp.float32)[EDGE - SUB :]
    head = short_conv(1, 0, SUB) * short_conv(2, 0, SUB)
    stacked = jnp.concatenate([head[:, cols] for cols in lanes], axis=0)
    own_head[...] = stacked.astype(jnp.bfloat16)
    gext[SUB : 2 * SUB] = head

    def send_head(i, carry):
        head_copy(me, n_seq - 1 - i).start()
        return carry

    lax.fori_loop(0, n_seq - 1 - me, send_head, 0)
    for copy in weight_copies[:2]:
        copy.start()

    queries[...] = short_conv(0, 0, rows)
    for cols in lanes:
        total = conv[:, cols]
        for j in range(SUB):
            total = total + gext[SUB + j : SUB + j + 1, cols] * fext[SUB - j : SUB - j + rows, cols]
        conv[:, cols] = total

    loads[6].wait()
    spans = jnp.exp(-float(rows) * rate[...])
    wide = jnp.broadcast_to(spans[:, None, :], (order, SUB, channels))

    def take_state(d, carry):
        held, front = carry
        state_copy(d, d).wait_recv()
        head_copy(d, d).wait_recv()
        stacked = heads[d].astype(jnp.float32)
        head = jnp.concatenate(
            [stacked[half * SUB : (half + 1) * SUB] for half in range(halves)], axis=1
        )
        return held * spans + states[d].astype(jnp.float32), front * wide + head[None]

    held, front = lax.fori_loop(
        0,
        me,
        take_state,
        (
            jnp.zeros((order, channels), jnp.float32),
            jnp.zeros((order, SUB, channels), jnp.float32),
        ),
    )

    for cols in lanes:
        rates = cube(rate[:, cols])
        decay = jnp.exp(-float(SUB) * rates)
        ahead = jnp.exp((step - float(rows - 1)) * rates) * front[:, :, cols]
        carried = amplitude_of(cols) * (held[:, cols] + jnp.sum(ahead, axis=1))
        term = cube(carried) * jnp.exp(-(step + 1.0) * rates)
        direct = skip[:, cols]
        for b in range(blocks):
            here = slice(b * SUB, (b + 1) * SUB)
            gated = gext[(b + 1) * SUB : (b + 2) * SUB, cols]
            total = conv[here, cols] + jnp.sum(term, axis=0)
            queries[here, cols] = queries[here, cols] * (total + direct * gated)
            if b < blocks - 1:
                term = term * decay
    hyena[...] = queries[...].astype(jnp.bfloat16)
    @pl.when(me > 0)
    def _():
        hyena_cross.start()

    hyena_twin.start()

    def product(rows_of, matrix, part, c):
        tile = matrix[part * channels : (part + 1) * channels, c * piece : (c + 1) * piece]
        return jnp.dot(rows_of[...], tile, preferred_element_type=jnp.float32)

    def send_cross(c):
        total = own_part[c] + product(twin_hyena, cross_weight, 1, c)
        cross_send[c] = total.astype(jnp.bfloat16)
        cross_copy(c).start()

    def finish(c, total):
        out_ref[:, c * piece : (c + 1) * piece] = total.astype(out_ref.dtype)

    def finish_cross(c):
        cross_copy(c).wait_recv()
        finish(c, own_part[c] + cross_recv[c].astype(jnp.float32))

    late = range(EARLY, CHUNKS)
    loads[7].wait()
    for c in range(CHUNKS):
        own_part[c] = product(hyena, cross_weight, 0, c)
    weight_copies[0].wait_recv()
    hyena_twin.wait_recv()
    for c in late:
        send_cross(c)

    @pl.when(me == 0)
    def _():
        for c in range(EARLY):
            send_cross(c)

    @pl.when(me > 0)
    def _():
        hyena_cross.wait_recv()
        hyena_far.start()

    loads[8].wait()
    weight_copies[1].wait_recv()
    for c in range(CHUNKS):
        own_part[c] = product(hyena, weight, 0, c) + product(twin_hyena, weight, 1, c)

    @pl.when(me > 0)
    def _():
        weight_copies[2].wait_recv()
        hyena_far.wait_recv()
        weight_copies[3].wait_recv()
        for c in range(EARLY):
            gathered = product(cross_hyena, far_weight, 0, c) + product(far_hyena, far_weight, 1, c)
            finish(c, own_part[c] + gathered)

    for c in late:
        finish_cross(c)

    @pl.when(me == 0)
    def _():
        for c in range(EARLY):
            finish_cross(c)
            cross_copy(c).wait_send()

    @pl.when(me > 0)
    def _():
        for copy in weight_copies[2:] + (hyena_cross, hyena_far):
            copy.wait_send()

    for c in late:
        cross_copy(c).wait_send()
    for copy in weight_copies[:2] + (hyena_twin,):
        copy.wait_send()

    @pl.when(me < n_seq - 1)
    def _():
        for i in (1, 2, 0):
            halo_copy(i).wait_send()

    def sent(d, carry):
        state_copy(me, d).wait_send()
        head_copy(me, d).wait_send()
        return carry

    lax.fori_loop(me + 1, n_seq, sent, 0)


def solution(mesh):
    n_seq, n_tp = mesh.shape["seq"], mesh.shape["tp"]
    assert n_tp == 4

    def local(query_in, key_in, value_in, short_weight, residue, rate, skip, out_weight):
        rows, channels = query_in.shape
        order, n_taps = rate.shape[0], short_weight.shape[1]
        width = out_weight.shape[1] // n_tp
        piece = width // CHUNKS
        f32, bf16 = jnp.float32, jnp.bfloat16
        pieces = pltpu.VMEM((CHUNKS, rows, piece), bf16)
        operands = (
            query_in,
            key_in,
            value_in,
            short_weight,
            residue,
            rate,
            skip.reshape(1, channels),
            out_weight,
        )
        return pl.pallas_call(
            functools.partial(kernel, n_seq, n_tp),
            out_shape=jax.ShapeDtypeStruct((rows, width), bf16),
            in_specs=[pl.BlockSpec(memory_space=pltpu.HBM)] * 8,
            out_specs=pl.BlockSpec(memory_space=pltpu.VMEM),
            scratch_shapes=[
                pltpu.VMEM((3, rows, channels), bf16),
                pltpu.VMEM((3, n_taps, channels), f32),
                pltpu.VMEM((order, channels), f32),
                pltpu.VMEM((order, channels), f32),
                pltpu.VMEM((1, channels), f32),
                pltpu.VMEM((2 * channels, width), bf16),
                pltpu.VMEM((2 * channels, width), bf16),
                pltpu.VMEM((2 * channels, EARLY * piece), bf16),
                pltpu.VMEM((3, EDGE, channels), bf16),
                pltpu.VMEM((3, rows + SUB, channels), f32),
                pltpu.VMEM((rows + SUB, channels), f32),
                pltpu.VMEM((rows + SUB, channels), f32),
                pltpu.VMEM((rows, channels), f32),
                pltpu.VMEM((n_seq, order, channels), bf16),
                pltpu.VMEM((order, channels), bf16),
                pltpu.VMEM((n_seq, SUB * channels // LANES, LANES), bf16),
                pltpu.VMEM((SUB * channels // LANES, LANES), bf16),
                pltpu.VMEM((rows, channels), f32),
                pltpu.VMEM((rows, channels), bf16),
                pltpu.VMEM((rows, channels), bf16),
                pltpu.VMEM((rows, channels), bf16),
                pltpu.VMEM((rows, channels), bf16),
                pieces,
                pieces,
                pltpu.VMEM((CHUNKS, rows, piece), f32),
                pltpu.SemaphoreType.DMA((9,)),
                pltpu.SemaphoreType.DMA((6,)),
                pltpu.SemaphoreType.DMA((n_seq,)),
                pltpu.SemaphoreType.DMA((n_seq,)),
                pltpu.SemaphoreType.DMA((n_seq,)),
                pltpu.SemaphoreType.DMA((n_seq,)),
                pltpu.SemaphoreType.DMA((7,)),
                pltpu.SemaphoreType.DMA((7,)),
                pltpu.SemaphoreType.DMA((CHUNKS,)),
                pltpu.SemaphoreType.DMA((CHUNKS,)),
            ],
            compiler_params=pltpu.CompilerParams(
                collective_id=0, has_side_effects=True, vmem_limit_bytes=40 * 1024 * 1024
            ),
        )(
            *[pltpu.with_memory_space_constraint(x, pltpu.HBM) for x in operands]
        )

    in_specs = (
        P("seq", "tp"),
        P("seq", "tp"),
        P("seq", "tp"),
        P(None, None, "tp"),
        P(None, "tp"),
        P(None, "tp"),
        P("tp"),
        P("tp", None),
    )
    return jax.shard_map(local, mesh=mesh, in_specs=in_specs, out_specs=P("seq", "tp"), check_vma=False)
```

```python
import functools

import jax
import jax.numpy as jnp
from jax import lax
from jax.experimental import pallas as pl
from jax.experimental.pallas import tpu as pltpu
from jax.sharding import PartitionSpec as P

MESH = pl.DeviceIdType.MESH
LANES = 128
SUB = 8
EDGE = 16
CHUNKS = 8
EARLY = 2


def one_minus_exp_neg(x):
    series = x * (1.0 - x * (1.0 / 2 - x * (1.0 / 6 - x * (1.0 / 24 - x * (1.0 / 120 - x * (1.0 / 720))))))
    return jnp.where(x < 0.2, series, 1.0 - jnp.exp(-x))


def kernel(
    n_seq,
    n_tp,
    query_hbm,
    key_hbm,
    value_hbm,
    taps_hbm,
    residue_hbm,
    rate_hbm,
    skip_hbm,
    weight_hbm,
    out_ref,
    streams,
    taps,
    residue,
    rate,
    skip,
    weight,
    cross_weight,
    far_weight,
    halo,
    extended,
    gext,
    fext,
    conv,
    states,
    own_state,
    heads,
    own_head,
    queries,
    hyena,
    twin_hyena,
    cross_hyena,
    far_hyena,
    cross_send,
    cross_recv,
    own_part,
    local_sem,
    halo_sem,
    state_send,
    state_recv,
    head_send,
    head_recv,
    tp_out,
    tp_in,
    cross_out,
    cross_in,
):
    rows, channels = query_hbm.shape
    order = rate_hbm.shape[0]
    n_taps = taps_hbm.shape[1]
    blocks = rows // SUB
    halves = channels // LANES
    width = out_ref.shape[1]
    piece = width // CHUNKS
    me = lax.axis_index("seq")
    tp = lax.axis_index("tp")
    twin = tp + 1 - 2 * lax.rem(tp, 2)
    cross = lax.rem(tp + 2, n_tp)
    twin_cross = lax.rem(twin + 2, n_tp)

    early = EARLY * piece

    def columns(block, first=0, count=width):
        return pl.ds(pl.multiple_of(block * width + first, piece), count)

    own_rows, twin_rows = pl.ds(0, channels), pl.ds(channels, channels)
    loads = [
        pltpu.make_async_copy(src, dst, local_sem.at[i])
        for i, (src, dst) in enumerate(
            (
                (rate_hbm, rate),
                (residue_hbm, residue),
                (key_hbm, streams.at[1]),
                (value_hbm, streams.at[2]),
                (taps_hbm, taps),
                (query_hbm, streams.at[0]),
                (skip_hbm, skip),
                (weight_hbm.at[:, columns(cross)], cross_weight.at[own_rows]),
                (weight_hbm.at[:, columns(tp)], weight.at[own_rows]),
            )
        )
    ]
    for load in loads:
        load.start()

    barrier = pltpu.get_barrier_semaphore()

    def greet(d, carry):
        pl.semaphore_signal(barrier, inc=1, device_id={"seq": d}, device_id_type=MESH)
        return carry

    lax.fori_loop(0, me, greet, 0)
    for partner in (twin, cross, twin_cross):
        pl.semaphore_signal(barrier, inc=1, device_id={"tp": partner}, device_id_type=MESH)

    step = lax.broadcasted_iota(jnp.int32, (order, SUB, LANES), 1).astype(jnp.float32)
    lanes = [slice(half * LANES, (half + 1) * LANES) for half in range(halves)]

    def cube(x):
        return jnp.broadcast_to(x[:, None, :], (order, SUB, LANES))

    def amplitude_of(cols):
        return residue[:, cols] * jnp.sqrt(one_minus_exp_neg(2.0 * rate[:, cols]))

    for load in loads[:2]:
        load.wait()
    fext[0:SUB] = jnp.zeros((SUB, channels), jnp.float32)
    for cols in lanes:
        rates = cube(rate[:, cols])
        decay = jnp.exp(-float(SUB) * rates)
        term = cube(amplitude_of(cols)) * jnp.exp(-step * rates)
        for b in range(blocks):
            fext[(b + 1) * SUB : (b + 2) * SUB, cols] = jnp.sum(term, axis=0)
            if b < blocks - 1:
                term = term * decay

    for load in loads[2:6]:
        load.wait()

    def short_conv(i, first, count):
        total = jnp.zeros((count, channels), jnp.float32)
        for t in range(n_taps):
            begin = first + SUB - t
            total = total + taps[i, t : t + 1, :] * extended[i, begin : begin + count]
        return total

    for i in range(3):
        extended[i, SUB:] = streams[i].astype(jnp.float32)
    gext[0 : 2 * SUB] = jnp.zeros((2 * SUB, channels), jnp.float32)
    gext[2 * SUB :] = short_conv(1, SUB, rows - SUB) * short_conv(2, SUB, rows - SUB)

    for cols in lanes:
        rates = cube(rate[:, cols])
        decay = jnp.exp(-float(SUB) * rates)
        total = jnp.broadcast_to(gext[2 * SUB : 3 * SUB, cols][None], (order, SUB, LANES))
        for b in range(2, blocks):
            total = total * decay + gext[(b + 1) * SUB : (b + 2) * SUB, cols][None]
        total = total * jnp.exp((step - float(SUB - 1)) * rates)
        own_state[:, cols] = jnp.sum(total, axis=1).astype(jnp.bfloat16)

    pl.semaphore_wait(barrier, n_seq - 1 - me + 3)

    def halo_copy(i):
        return pltpu.make_async_remote_copy(
            src_ref=streams.at[i, pl.ds(rows - EDGE, EDGE)],
            dst_ref=halo.at[i],
            send_sem=halo_sem.at[i],
            recv_sem=halo_sem.at[3 + i],
            device_id={"seq": lax.rem(me + 1, n_seq)},
            device_id_type=MESH,
        )

    def state_copy(slot, d):
        return pltpu.make_async_remote_copy(
            src_ref=own_state,
            dst_ref=states.at[slot],
            send_sem=state_send.at[d],
            recv_sem=state_recv.at[slot],
            device_id={"seq": d},
            device_id_type=MESH,
        )

    def head_copy(slot, d):
        return pltpu.make_async_remote_copy(
            src_ref=own_head,
            dst_ref=heads.at[slot],
            send_sem=head_send.at[d],
            recv_sem=head_recv.at[slot],
            device_id={"seq": d},
            device_id_type=MESH,
        )

    def tp_copy(i, src, dst, target):
        return pltpu.make_async_remote_copy(
            src_ref=src,
            dst_ref=dst,
            send_sem=tp_out.at[i],
            recv_sem=tp_in.at[i],
            device_id={"tp": target},
            device_id_type=MESH,
        )

    weight_copies = (
        tp_copy(
            0,
            weight_hbm.at[:, columns(twin_cross)],
            cross_weight.at[twin_rows],
            twin,
        ),
        tp_copy(1, weight_hbm.at[:, columns(twin)], weight.at[twin_rows], twin),
        tp_copy(2, weight_hbm.at[:, columns(cross, 0, early)], far_weight.at[own_rows], cross),
        tp_copy(
            3,
            weight_hbm.at[:, columns(twin_cross, 0, early)],
            far_weight.at[twin_rows],
            twin_cross,
        ),
    )
    hyena_cross = tp_copy(4, hyena, cross_hyena, cross)
    hyena_twin = tp_copy(5, hyena, twin_hyena, twin)
    hyena_far = tp_copy(6, cross_hyena, far_hyena, twin)

    def cross_copy(c):
        return pltpu.make_async_remote_copy(
            src_ref=cross_send.at[c],
            dst_ref=cross_recv.at[c],
            send_sem=cross_out.at[c],
            recv_sem=cross_in.at[c],
            device_id={"tp": cross},
            device_id_type=MESH,
        )

    @pl.when(me < n_seq - 1)
    def _():
        for i in (1, 2, 0):
            halo_copy(i).start()

    def send_state(i, carry):
        state_copy(me, n_seq - 1 - i).start()
        return carry

    lax.fori_loop(0, n_seq - 1 - me, send_state, 0)
    @pl.when(me > 0)
    def _():
        for copy in weight_copies[2:]:
            copy.start()


    def local_conv(half, carry):
        cols = pl.ds(pl.multiple_of(half * LANES, LANES), LANES)
        total = jnp.zeros((rows, LANES), jnp.float32)
        for s in range(SUB):
            shifted = gext[SUB - s : SUB - s + rows, cols]
            for q in range(blocks):
                tap = fext[(q + 1) * SUB + s : (q + 1) * SUB + s + 1, cols]
                if q == 0:
                    total = total + tap * shifted
                else:
                    lower = total[q * SUB :] + tap * shifted[: rows - q * SUB]
                    total = jnp.concatenate([total[: q * SUB], lower], axis=0)
        conv[:, cols] = total
        return carry

    lax.fori_loop(0, halves, local_conv, 0)

    @pl.when(me == 0)
    def _():
        halo[...] = jnp.zeros_like(halo)

    @pl.when(me > 0)
    def _():
        for i in (1, 2, 0):
            halo_copy(i).wait_recv()

    for i in range(3):
        extended[i, 0:SUB] = halo[i].astype(jnp.float32)[EDGE - SUB :]
    head = short_conv(1, 0, SUB) * short_conv(2, 0, SUB)
    stacked = jnp.concatenate([head[:, cols] for cols in lanes], axis=0)
    own_head[...] = stacked.astype(jnp.bfloat16)
    gext[SUB : 2 * SUB] = head

    def send_head(i, carry):
        head_copy(me, n_seq - 1 - i).start()
        return carry

    lax.fori_loop(0, n_seq - 1 - me, send_head, 0)
    for copy in weight_copies[:2]:
        copy.start()

    queries[...] = short_conv(0, 0, rows)
    for cols in lanes:
        total = conv[:, cols]
        for j in range(SUB):
            total = total + gext[SUB + j : SUB + j + 1, cols] * fext[SUB - j : SUB - j + rows, cols]
        conv[:, cols] = total

    loads[6].wait()
    spans = jnp.exp(-float(rows) * rate[...])
    wide = jnp.broadcast_to(spans[:, None, :], (order, SUB, channels))

    def take_state(d, carry):
        held, front = carry
        state_copy(d, d).wait_recv()
        head_copy(d, d).wait_recv()
        stacked = heads[d].astype(jnp.float32)
        head = jnp.concatenate(
            [stacked[half * SUB : (half + 1) * SUB] for half in range(halves)], axis=1
        )
        return held * spans + states[d].astype(jnp.float32), front * wide + head[None]

    held, front = lax.fori_loop(
        0,
        me,
        take_state,
        (
            jnp.zeros((order, channels), jnp.float32),
            jnp.zeros((order, SUB, channels), jnp.float32),
        ),
    )

    for cols in lanes:
        rates = cube(rate[:, cols])
        decay = jnp.exp(-float(SUB) * rates)
        ahead = jnp.exp((step - float(rows - 1)) * rates) * front[:, :, cols]
        carried = amplitude_of(cols) * (held[:, cols] + jnp.sum(ahead, axis=1))
        term = cube(carried) * jnp.exp(-(step + 1.0) * rates)
        direct = skip[:, cols]
        for b in range(blocks):
            here = slice(b * SUB, (b + 1) * SUB)
            gated = gext[(b + 1) * SUB : (b + 2) * SUB, cols]
            total = conv[here, cols] + jnp.sum(term, axis=0)
            queries[here, cols] = queries[here, cols] * (total + direct * gated)
            if b < blocks - 1:
                term = term * decay
    hyena[...] = queries[...].astype(jnp.bfloat16)
    @pl.when(me > 0)
    def _():
        hyena_cross.start()

    hyena_twin.start()

    def product(rows_of, matrix, part, c):
        tile = matrix[part * channels : (part + 1) * channels, c * piece : (c + 1) * piece]
        return jnp.dot(rows_of[...], tile, preferred_element_type=jnp.float32)

    def send_cross(c):
        total = own_part[c] + product(twin_hyena, cross_weight, 1, c)
        cross_send[c] = total.astype(jnp.bfloat16)
        cross_copy(c).start()

    def finish(c, total):
        out_ref[:, c * piece : (c + 1) * piece] = total.astype(out_ref.dtype)

    def finish_cross(c):
        cross_copy(c).wait_recv()
        finish(c, own_part[c] + cross_recv[c].astype(jnp.float32))

    late = range(EARLY, CHUNKS)
    loads[7].wait()
    for c in range(CHUNKS):
        own_part[c] = product(hyena, cross_weight, 0, c)
    weight_copies[0].wait_recv()
    hyena_twin.wait_recv()
    for c in late:
        send_cross(c)

    @pl.when(me == 0)
    def _():
        for c in range(EARLY):
            send_cross(c)

    @pl.when(me > 0)
    def _():
        hyena_cross.wait_recv()
        hyena_far.start()

    loads[8].wait()
    weight_copies[1].wait_recv()
    for c in range(CHUNKS):
        own_part[c] = product(hyena, weight, 0, c) + product(twin_hyena, weight, 1, c)

    @pl.when(me > 0)
    def _():
        weight_copies[2].wait_recv()
        hyena_far.wait_recv()
        weight_copies[3].wait_recv()
        for c in range(EARLY):
            gathered = product(cross_hyena, far_weight, 0, c) + product(far_hyena, far_weight, 1, c)
            finish(c, own_part[c] + gathered)

    for c in late:
        finish_cross(c)

    @pl.when(me == 0)
    def _():
        for c in range(EARLY):
            finish_cross(c)
            cross_copy(c).wait_send()

    @pl.when(me > 0)
    def _():
        for copy in weight_copies[2:] + (hyena_cross, hyena_far):
            copy.wait_send()

    for c in late:
        cross_copy(c).wait_send()
    for copy in weight_copies[:2] + (hyena_twin,):
        copy.wait_send()

    @pl.when(me < n_seq - 1)
    def _():
        for i in (1, 2, 0):
            halo_copy(i).wait_send()

    def sent(d, carry):
        state_copy(me, d).wait_send()
        head_copy(me, d).wait_send()
        return carry

    lax.fori_loop(me + 1, n_seq, sent, 0)


def solution(mesh):
    n_seq, n_tp = mesh.shape["seq"], mesh.shape["tp"]
    assert n_tp == 4

    def local(query_in, key_in, value_in, short_weight, residue, rate, skip, out_weight):
        rows, channels = query_in.shape
        order, n_taps = rate.shape[0], short_weight.shape[1]
        width = out_weight.shape[1] // n_tp
        piece = width // CHUNKS
        f32, bf16 = jnp.float32, jnp.bfloat16
        pieces = pltpu.VMEM((CHUNKS, rows, piece), bf16)
        operands = (
            query_in,
            key_in,
            value_in,
            short_weight,
            residue,
            rate,
            skip.reshape(1, channels),
            out_weight,
        )
        return pl.pallas_call(
            functools.partial(kernel, n_seq, n_tp),
            out_shape=jax.ShapeDtypeStruct((rows, width), bf16),
            in_specs=[pl.BlockSpec(memory_space=pltpu.HBM)] * 8,
            out_specs=pl.BlockSpec(memory_space=pltpu.VMEM),
            scratch_shapes=[
                pltpu.VMEM((3, rows, channels), bf16),
                pltpu.VMEM((3, n_taps, channels), f32),
                pltpu.VMEM((order, channels), f32),
                pltpu.VMEM((order, channels), f32),
                pltpu.VMEM((1, channels), f32),
                pltpu.VMEM((2 * channels, width), bf16),
                pltpu.VMEM((2 * channels, width), bf16),
                pltpu.VMEM((2 * channels, EARLY * piece), bf16),
                pltpu.VMEM((3, EDGE, channels), bf16),
                pltpu.VMEM((3, rows + SUB, channels), f32),
                pltpu.VMEM((rows + SUB, channels), f32),
                pltpu.VMEM((rows + SUB, channels), f32),
                pltpu.VMEM((rows, channels), f32),
                pltpu.VMEM((n_seq, order, channels), bf16),
                pltpu.VMEM((order, channels), bf16),
                pltpu.VMEM((n_seq, SUB * channels // LANES, LANES), bf16),
                pltpu.VMEM((SUB * channels // LANES, LANES), bf16),
                pltpu.VMEM((rows, channels), f32),
                pltpu.VMEM((rows, channels), bf16),
                pltpu.VMEM((rows, channels), bf16),
                pltpu.VMEM((rows, channels), bf16),
                pltpu.VMEM((rows, channels), bf16),
                pieces,
                pieces,
                pltpu.VMEM((CHUNKS, rows, piece), f32),
                pltpu.SemaphoreType.DMA((9,)),
                pltpu.SemaphoreType.DMA((6,)),
                pltpu.SemaphoreType.DMA((n_seq,)),
                pltpu.SemaphoreType.DMA((n_seq,)),
                pltpu.SemaphoreType.DMA((n_seq,)),
                pltpu.SemaphoreType.DMA((n_seq,)),
                pltpu.SemaphoreType.DMA((7,)),
                pltpu.SemaphoreType.DMA((7,)),
                pltpu.SemaphoreType.DMA((CHUNKS,)),
                pltpu.SemaphoreType.DMA((CHUNKS,)),
            ],
            compiler_params=pltpu.CompilerParams(
                collective_id=0, has_side_effects=True, vmem_limit_bytes=40 * 1024 * 1024
            ),
        )(
            *[pltpu.with_memory_space_constraint(x, pltpu.HBM) for x in operands]
        )

    in_specs = (
        P("seq", "tp"),
        P("seq", "tp"),
        P("seq", "tp"),
        P(None, None, "tp"),
        P(None, "tp"),
        P(None, "tp"),
        P("tp"),
        P("tp", None),
    )
    return jax.shard_map(local, mesh=mesh, in_specs=in_specs, out_specs=P("seq", "tp"), check_vma=False)
```
